256 devices in a mesh: dp: 8 (over x, core), feat: 32 (over z, y).
Axes of the slice: x: 4, y: 4, z: 8, core: 2. Of those that a mesh axis runs over, the one named last changes fastest.
Arguments:
- feature_table: bfloat16 [768, 32768], P('feat'), may hold values from -6 to 6
- node_ids: int32 [131072], P('dp'), may hold values from 0 to 32767
- hop_cols: int32 [256, 8], P('dp'), may hold values from 0 to 127
- hop_tiles: bfloat16 [256, 8, 128, 128], P('dp'), may hold values from -0.1875 to 0.1875
- target_cols: int32 [64, 8], P('dp'), may hold values from 0 to 31
- target_tiles: bfloat16 [64, 8, 128, 128], P('dp'), may hold values from -0.1875 to 0.1875
- self_weight: bfloat16 [768, 1024], P('feat'), may hold values from -0.21875 to 0.21875
- neigh_weight: bfloat16 [768, 1024], P('feat'), may hold values from -0.21875 to 0.21875
- hidden_bias: float32 [1024], P('feat'), may hold values from -3 to 3
- head_self: bfloat16 [1024, 153], P('feat'), may hold values from -0.25 to 0.25
- head_neigh: bfloat16 [1024, 153], P('feat'), may hold values from -0.25 to 0.25
- batch_sizes: int32 [8], replicated, may hold values from 256 to 1024, as said below
- logit_cotangent: bfloat16 [153, 8192], P(None, 'dp'), may hold values from -6 to 6
Outputs:
- logits: float32 [153, 8192], P(None, 'dp')
- grad_self: float32 [768, 1024], P('feat')
- grad_neigh: float32 [768, 1024], P('feat')
- grad_head_self: float32 [1024, 153], P('feat')
- grad_head_neigh: float32 [1024, 153], P('feat')
- grad_bias: float32 [1024], P('feat')
The draws below stay inside these ranges and needn't reach their ends.
Inputs may be any that keep to these rules, and one draw needn't show every extreme that they name: `batch_sizes`: at least one mini-batch has exactly 1024 live targets.
All inputs are finite; a program needn't handle non-finite values.
Results may differ from the reference program's by a relative error of at most 0.024.
The reference program's roundings to bfloat16 on the way (of `features`, `first_agg`, `hidden`, `second_agg`, `cot`, `back_agg` and `dpre_low`) count: a program that leaves them out, or rounds other values in their place, can miss the bound.
Values may be sent and summed in bfloat16 or wider, within the bound.
No kernel may reach another device: no remote copies, remote signals or barrier semaphores. Data moves between devices by JAX's collectives and lax.ppermute only.
A program may use at most 128 MiB of HBM per device.

```python
import jax
import jax.numpy as jnp

F = 768
H = 1024
C = 153
TILE = 128
K1 = 8
K2 = 8
N1 = 4096
TABLE = 32768
N2 = 16384
BATCH = 1024
N_DP = 8


def draw_batch_sizes(key, part):
    key = jax.random.fold_in(key, 11)
    first_key, second_key = jax.random.split(key)
    counts = jax.random.randint(first_key, (N_DP,), BATCH // 4, BATCH + 1)
    filled = jax.random.randint(second_key, (), 0, N_DP)
    return jnp.where(jnp.arange(N_DP) == filled, BATCH, counts).astype(jnp.int32)


def touch_ends(array, rng, smallest, largest):
    longest = array.shape.index(max(array.shape))
    spots = []
    for shift in (0, 1):
        where = [jax.random.randint(jax.random.fold_in(rng, axis), (), 0, length) for axis, length in enumerate(array.shape)]
        where[longest] = (where[longest] + shift) % array.shape[longest]
        spots.append(tuple(where))
    return array.at[spots[0]].set(smallest).at[spots[1]].set(largest)


def level_of(own_key, extent, cuts, low, high):
    loudness = 1.0
    for position, parts in cuts:
        heights = jax.random.uniform(jax.random.fold_in(jax.random.fold_in(own_key, 6), position), (parts,), jnp.float32, low / len(cuts), high / len(cuts))
        loudness = loudness * jnp.repeat(jnp.exp(heights), extent[position] // parts).reshape((-1,) + (1,) * (len(extent) - 1 - position))
    return loudness


def centred(key, dims, scale, reach, shards=(), dtype=jnp.bfloat16):
    values = jax.random.normal(key, dims, jnp.float32) * scale
    if len(shards) > 0:
        values = level_of(key, dims, shards, -0.22, 0.18) * values
    return jnp.clip(values, min=-reach, max=reach).astype(dtype)


def setup_inputs(seed: int = 0) -> dict:
    arg_keys = jax.random.split(jax.random.key(seed), 14)
    return {
        "feature_table": centred(arg_keys[0], (F, TABLE), 1.0, 6.0, ((0, 32),)),
        "node_ids": touch_ends(jax.random.randint(arg_keys[1], (N_DP * N2,), 0, TABLE), jax.random.fold_in(arg_keys[1], 1), 0, TABLE - 1).astype(jnp.int32),
        "hop_cols": touch_ends(jax.random.randint(arg_keys[2], (N_DP * (N1 // TILE), K1), 0, N2 // TILE), jax.random.fold_in(arg_keys[2], 1), 0, (N2 // TILE) - 1).astype(jnp.int32),
        "hop_tiles": centred(arg_keys[3], (N_DP * (N1 // TILE), K1, TILE, TILE), (K1 * TILE) ** -0.5, 0.1875, ((0, 8),)),
        "target_cols": touch_ends(jax.random.randint(arg_keys[4], (N_DP * (BATCH // TILE), K2), 0, N1 // TILE), jax.random.fold_in(arg_keys[4], 1), 0, (N1 // TILE) - 1).astype(jnp.int32),
        "target_tiles": centred(arg_keys[5], (N_DP * (BATCH // TILE), K2, TILE, TILE), (K2 * TILE) ** -0.5, 0.1875, ((0, 8),)),
        "self_weight": centred(arg_keys[6], (F, H), F ** -0.5, 0.21875, ((0, 32),)),
        "neigh_weight": centred(arg_keys[7], (F, H), F ** -0.5, 0.21875, ((0, 32),)),
        "hidden_bias": centred(arg_keys[8], (H,), 0.5, 3.0, ((0, 32),), jnp.float32),
        "head_self": centred(arg_keys[9], (H, C), (H // 2) ** -0.5, 0.25, ((0, 32),)),
        "head_neigh": centred(arg_keys[10], (H, C), (H // 2) ** -0.5, 0.25, ((0, 32),)),
        "batch_sizes": draw_batch_sizes(jax.random.fold_in(arg_keys[13], 71), 0),
        "logit_cotangent": centred(arg_keys[12], (C, N_DP * BATCH), 1.0, 6.0, ((1, 8),)),
    }


def aggregate(source, tile_cols, tile_vals):
    width = tile_vals.shape[-1]
    blocks = source.reshape(source.shape[0], -1, width)
    chosen = blocks[:, tile_cols]
    merged = jnp.einsum("pmkj,mkij->pmi", chosen.astype(jnp.float32), tile_vals.astype(jnp.float32))
    return merged.reshape(source.shape[0], -1)


def spread_back(grads, tile_cols, tile_vals, count):
    width = tile_vals.shape[-1]
    shaped = grads.reshape(grads.shape[0], -1, width).astype(jnp.float32)
    pieces = jnp.einsum("pmi,mkij->pmkj", shaped, tile_vals.astype(jnp.float32))
    total = jnp.zeros((grads.shape[0], count, width), jnp.float32).at[:, tile_cols].add(pieces)
    return total.reshape(grads.shape[0], -1)


def reference(feature_table, node_ids, hop_cols, hop_tiles, target_cols, target_tiles, self_weight, neigh_weight, hidden_bias, head_self, head_neigh, batch_sizes, logit_cotangent):
    first_blocks = N1 // TILE
    target_blocks = BATCH // TILE
    grad_self = jnp.zeros((F, H), jnp.float32)
    grad_neigh = jnp.zeros((F, H), jnp.float32)
    grad_head_self = jnp.zeros((H, C), jnp.float32)
    grad_head_neigh = jnp.zeros((H, C), jnp.float32)
    grad_bias = jnp.zeros((H,), jnp.float32)
    score_list = []
    for member in range(N_DP):
        member_ids = node_ids[member * N2:(member + 1) * N2]
        features = jnp.take(feature_table, member_ids, axis=1)
        own_rows = features[:, :N1]
        hop_c = hop_cols[member * first_blocks:(member + 1) * first_blocks]
        hop_t = hop_tiles[member * first_blocks:(member + 1) * first_blocks]
        tgt_c = target_cols[member * target_blocks:(member + 1) * target_blocks]
        tgt_t = target_tiles[member * target_blocks:(member + 1) * target_blocks]
        first_agg = aggregate(features, hop_c, hop_t).astype(jnp.bfloat16)
        preact = jnp.dot(self_weight.T, own_rows, preferred_element_type=jnp.float32)
        preact = preact + jnp.dot(neigh_weight.T, first_agg, preferred_element_type=jnp.float32)
        preact = preact + hidden_bias[:, None]
        hidden = jnp.maximum(preact, 0.0).astype(jnp.bfloat16)
        second_agg = aggregate(hidden, tgt_c, tgt_t).astype(jnp.bfloat16)
        targets = hidden[:, :BATCH]
        scores = jnp.dot(head_self.T, targets, preferred_element_type=jnp.float32)
        scores = scores + jnp.dot(head_neigh.T, second_agg, preferred_element_type=jnp.float32)
        score_list.append(scores)
        member_cot = logit_cotangent[:, member * BATCH:(member + 1) * BATCH]
        live = jnp.arange(BATCH)[None, :] < batch_sizes[member]
        cot = jnp.where(live, member_cot, jnp.zeros_like(member_cot))
        back_agg = jnp.dot(head_neigh, cot, preferred_element_type=jnp.float32).astype(jnp.bfloat16)
        direct = jnp.dot(head_self, cot, preferred_element_type=jnp.float32)
        dhidden = spread_back(back_agg, tgt_c, tgt_t, first_blocks)
        dhidden = dhidden.at[:, :BATCH].add(direct)
        dpre = jnp.where(preact > 0.0, dhidden, jnp.zeros_like(dhidden))
        dpre_low = dpre.astype(jnp.bfloat16)
        grad_bias = grad_bias + jnp.sum(dpre, axis=1)
        grad_self = grad_self + jnp.dot(own_rows, dpre_low.T, preferred_element_type=jnp.float32)
        grad_neigh = grad_neigh + jnp.dot(first_agg, dpre_low.T, preferred_element_type=jnp.float32)
        grad_head_self = grad_head_self + jnp.dot(targets, cot.T, preferred_element_type=jnp.float32)
        grad_head_neigh = grad_head_neigh + jnp.dot(second_agg, cot.T, preferred_element_type=jnp.float32)
    logits = jnp.concatenate(score_list, axis=1)
    return (logits, grad_self, grad_neigh, grad_head_self, grad_head_neigh, grad_bias)
```

```python
import jax
import jax.numpy as jnp
from jax import lax
from jax.experimental import pallas as pl
from jax.experimental.pallas import tpu as pltpu
from jax.sharding import Mesh, PartitionSpec as P

TILE = 128
FEAT = ("z", "y")
DP = ("x", "core")
CLS = 192
BF = jnp.bfloat16
F32 = jnp.float32
NT = (((1,), (1,)), ((), ()))
VMEM = pl.BlockSpec(memory_space=pltpu.VMEM)
SMEM = pl.BlockSpec(memory_space=pltpu.SMEM)
HBM = pl.BlockSpec(memory_space=pl.ANY)
LIMIT = pltpu.CompilerParams(vmem_limit_bytes=56 * 2**20)


def aligned(index, size):
    return pl.ds(pl.multiple_of(index * size, size), size)


def hop_kernel(ids, cols, table, tiles_hbm, out, rows, picked, tiles, sem):
    width = table.shape[0]
    blocks = tiles.shape[0]
    group = blocks // 8
    copies = [
        pltpu.make_async_copy(
            tiles_hbm.at[pl.ds(j * group, group)], tiles.at[pl.ds(j * group, group)], sem.at[j]
        )
        for j in range(8)
    ]
    for copy in copies:
        copy.start()

    def turn(b, carry):
        rows[aligned(b, TILE), 0:width] = table[:, aligned(b, TILE)].astype(F32).T
        return carry

    lax.fori_loop(0, table.shape[1] // TILE, turn, 0, unroll=8)
    step = 64

    def pick(g, carry):
        base = pl.multiple_of(g * step, step)
        for u in range(step):
            picked[pl.ds(base + u, 1), :] = rows[pl.ds(ids[base + u], 1), :]
        return carry

    lax.fori_loop(0, ids.shape[0] // step, pick, 0)
    for copy in copies:
        copy.wait()

    def merge(r, carry):
        out[r, 0:width, :] = picked[aligned(r, TILE), :].T[0:width].astype(BF)
        left = jnp.concatenate([tiles[r, k] for k in range(8)], axis=1)
        right = jnp.concatenate(
            [picked[aligned(cols[r * 8 + k], TILE), :].astype(BF) for k in range(8)], axis=0
        )
        total = jnp.dot(left, right, preferred_element_type=F32)
        out[r, width : 2 * width, :] = total.T[0:width].astype(BF)
        return carry

    lax.fori_loop(0, blocks, merge, 0, unroll=2)


def hop(table, ids, cols, tiles):
    blocks = tiles.shape[0]
    return pl.pallas_call(
        hop_kernel,
        in_specs=[SMEM, SMEM, VMEM, HBM],
        out_specs=VMEM,
        scratch_shapes=[
            pltpu.VMEM((table.shape[1], TILE), F32),
            pltpu.VMEM((ids.shape[0], TILE), F32),
            pltpu.VMEM(tiles.shape, BF),
            pltpu.SemaphoreType.DMA((8,)),
        ],
        out_shape=jax.ShapeDtypeStruct((blocks, 2 * table.shape[0], TILE), BF),
        compiler_params=LIMIT,
        cost_estimate=pl.CostEstimate(flops=10**9, bytes_accessed=60 * 10**6, transcendentals=0),
    )(ids, cols.reshape(-1), table, tiles)


def spread_kernel(cols, back, direct, tiles, out):
    out[...] = jnp.zeros_like(out)
    for r in range(tiles.shape[0]):
        out[r] = direct[:, r * TILE : (r + 1) * TILE]
    for r in range(tiles.shape[0]):
        part = back[:, r * TILE : (r + 1) * TILE]
        for k in range(8):
            out[cols[r * 8 + k]] += jnp.dot(part, tiles[r, k], preferred_element_type=F32)


def spread(cols, back, direct, tiles, blocks):
    return pl.pallas_call(
        spread_kernel,
        in_specs=[SMEM, VMEM, VMEM, VMEM],
        out_specs=VMEM,
        out_shape=jax.ShapeDtypeStruct((blocks, back.shape[0], TILE), F32),
        compiler_params=LIMIT,
    )(cols.reshape(-1), back, direct, tiles)


def last_kernel(
    place, cols, hidden, dhidden, feats, tiles, cot, self_t, neigh_t, out, heads, second, total, bias
):
    y = place[0]
    groups, blocks, deep, _ = feats.shape
    own = pl.ds(pl.multiple_of(y * 32, 32), 32)
    for r in range(tiles.shape[0]):
        left = jnp.concatenate([hidden[cols[r * 8 + k]] for k in range(8)], axis=1)
        right = jnp.concatenate([tiles[r, k] for k in range(8)], axis=1)
        second[r] = lax.dot_general(left, right, NT, preferred_element_type=F32).astype(BF)
    for half in range(2):
        at = 2 * y + half
        scores = jnp.dot(self_t[...], hidden[at], preferred_element_type=F32)
        scores = scores + jnp.dot(neigh_t[...], second[at], preferred_element_type=F32)
        for z in range(groups):
            out[z, deep + 24 * half : deep + 24 * (half + 1), :] = scores[24 * z : 24 * (z + 1)]
    total[...] = jnp.zeros_like(total)
    bias[...] = jnp.zeros_like(bias)

    def grow(b, carry):
        kept = jnp.where(hidden[b].astype(F32) > 0.0, dhidden[b], 0.0)
        low = kept.astype(BF)
        stack = jnp.concatenate([feats[z, b] for z in range(groups)], axis=0)
        total[...] += lax.dot_general(stack, low, NT, preferred_element_type=F32)
        bias[...] += kept
        return carry

    lax.fori_loop(0, blocks, grow, 0, unroll=4)
    for z in range(groups):
        out[z, 0:deep, :] = total[z * deep : (z + 1) * deep]
    targets = jnp.concatenate([hidden[r, own, :] for r in range(tiles.shape[0])], axis=1)
    merged = jnp.concatenate([second[r, own, :] for r in range(tiles.shape[0])], axis=1)
    mine = jnp.sum(bias[own, :], axis=1, keepdims=True)
    lane = lax.broadcasted_iota(jnp.int32, (32, 256), 1)
    grad = lax.dot_general(targets, cot[...], NT, preferred_element_type=F32)
    heads[:, 0:256] = jnp.where(lane == 255, mine, grad)
    heads[:, 256:512] = lax.dot_general(merged, cot[...], NT, preferred_element_type=F32)


def last(place, cols, hidden, dhidden, feats, tiles, cot, self_t, neigh_t):
    groups, blocks, deep, _ = feats.shape
    return pl.pallas_call(
        last_kernel,
        in_specs=[SMEM, SMEM] + [VMEM] * 7,
        out_specs=[VMEM, VMEM],
        scratch_shapes=[
            pltpu.VMEM((tiles.shape[0], TILE, TILE), BF),
            pltpu.VMEM((groups * deep, TILE), F32),
            pltpu.VMEM((TILE, TILE), F32),
        ],
        out_shape=[
            jax.ShapeDtypeStruct((groups, deep + 48, TILE), F32),
            jax.ShapeDtypeStruct((32, 512), F32),
        ],
        compiler_params=LIMIT,
    )(place, cols.reshape(-1), hidden, dhidden, feats, tiles, cot, self_t, neigh_t)


def swap_core(value):
    return lax.ppermute(value, "core", [(0, 1), (1, 0)])


def sum_dp(value):
    value = value + swap_core(value)
    value = value + lax.ppermute(value, "x", [(0, 1), (1, 0), (2, 3), (3, 2)])
    return value + lax.ppermute(value, "x", [(0, 3), (3, 0), (1, 2), (2, 1)])


def shards(
    feature_table,
    node_ids,
    hop_cols,
    hop_tiles,
    target_cols,
    target_tiles,
    self_weight,
    neigh_weight,
    hidden_bias,
    head_self,
    head_neigh,
    batch_sizes,
    logit_cotangent,
):
    blocks = hop_cols.shape[0]
    classes, target_rows = logit_cotangent.shape
    first_core = lax.axis_index("core") == 0
    y = lax.axis_index("y")

    mine = lax.all_gather(
        jnp.where(first_core, self_weight, neigh_weight), FEAT, axis=0, tiled=True
    )
    other = swap_core(mine)

    every_bias = lax.all_to_all(
        jnp.broadcast_to(hidden_bias[None, None], (32, 1, 32)), FEAT, 0, 0, tiled=True
    ).reshape(-1)
    pair = jnp.concatenate([head_self, head_neigh], axis=1)
    pair = lax.all_to_all(
        jnp.broadcast_to(pair[None], (4,) + pair.shape), "y", 0, 0, tiled=True
    ).reshape(TILE, 2 * classes)
    heads_self, heads_neigh = pair[:, :classes], pair[:, classes:]

    live_count = batch_sizes[lax.axis_index("x") * 2 + lax.axis_index("core")]
    live = jnp.arange(target_rows)[None, :] < live_count
    cot = jnp.where(live, logit_cotangent, jnp.zeros_like(logit_cotangent))
    back_agg = jnp.dot(heads_neigh, cot, preferred_element_type=F32).astype(BF)
    direct = jnp.dot(heads_self, cot, preferred_element_type=F32)
    dhidden = spread(target_cols, back_agg, direct, target_tiles, blocks)

    send = hop(feature_table, node_ids, hop_cols, hop_tiles)
    feats = lax.all_gather(send, "z", axis=0, tiled=False)
    got = lax.all_to_all(send, FEAT, 0, 0, tiled=True)
    deep = feature_table.shape[0]
    own_rows = got[:, :deep].reshape(-1, TILE)
    first_agg = got[:, deep:].reshape(-1, TILE)
    with_mine = jnp.where(first_core, own_rows, first_agg)
    with_other = jnp.where(first_core, first_agg, own_rows)
    preact = jnp.dot(mine.T, with_mine, preferred_element_type=F32)
    preact = preact + jnp.dot(other.T, with_other, preferred_element_type=F32)
    preact = preact + every_bias[:, None]
    hidden = jnp.maximum(preact, 0.0).astype(BF)
    hidden = jnp.broadcast_to(hidden.reshape(8, 1, TILE, TILE), (8, 4, TILE, TILE))
    hidden = lax.all_to_all(hidden.reshape(32, TILE, TILE), FEAT, 0, 0, tiled=True)

    pad = ((0, CLS - classes), (0, 0))
    out, heads = last(
        y.reshape(1),
        target_cols,
        hidden,
        dhidden,
        feats,
        target_tiles,
        jnp.pad(cot, ((0, 256 - classes), (0, 0))),
        jnp.pad(heads_self.T, pad),
        jnp.pad(heads_neigh.T, pad),
    )
    out = lax.all_to_all(out, "z", 0, 0, tiled=True)
    scores = jnp.sum(out[:, 2 * deep :], axis=0).astype(BF)
    scores = lax.all_to_all(
        jnp.broadcast_to(scores[None], (32,) + scores.shape), FEAT, 0, 0, tiled=True
    )
    scores = scores.reshape(8, 4, 2, 24, TILE).transpose(0, 3, 1, 2, 4).reshape(CLS, target_rows)
    logits = scores[:classes].astype(F32)

    packed = jnp.concatenate(
        [out[:, : 2 * deep].reshape(-1, TILE), heads.reshape(-1, TILE)], axis=0
    )
    packed = sum_dp(packed)
    grads = packed[: 16 * deep].reshape(8, 2, deep, TILE).transpose(1, 2, 0, 3)
    grads = grads.reshape(2, deep, 8 * TILE)
    heads = packed[16 * deep :].reshape(32, 512)
    return (
        logits,
        grads[0],
        grads[1],
        heads[:, :classes],
        heads[:, 256 : 256 + classes],
        heads[:, 255],
    )


def solution(mesh):
    split = Mesh(mesh.devices.reshape(4, 2, 8, 4), DP + FEAT)
    return jax.shard_map(
        shards,
        mesh=split,
        in_specs=(
            P(FEAT, None),
            P(DP),
            P(DP, None),
            P(DP, None, None, None),
            P(DP, None),
            P(DP, None, None, None),
            P(FEAT, None),
            P(FEAT, None),
            P(FEAT),
            P(FEAT, None),
            P(FEAT, None),
            P(),
            P(None, DP),
        ),
        out_specs=(
            P(None, DP),
            P(FEAT, None),
            P(FEAT, None),
            P(FEAT, None),
            P(FEAT, None),
            P(FEAT),
        ),
        check_vma=False,
    )
```

```python
import jax
import jax.numpy as jnp
from jax import lax
from jax.experimental import pallas as pl
from jax.experimental.pallas import tpu as pltpu
from jax.sharding import Mesh, PartitionSpec as P

TILE = 128
FEAT = ("z", "y")
DP = ("x", "core")
BF = jnp.bfloat16
F32 = jnp.float32
NT = (((1,), (1,)), ((), ()))
VMEM = pl.BlockSpec(memory_space=pltpu.VMEM)
SMEM = pl.BlockSpec(memory_space=pltpu.SMEM)
HBM = pl.BlockSpec(memory_space=pl.ANY)
LIMIT = pltpu.CompilerParams(vmem_limit_bytes=56 * 2**20)


def aligned(index, size):
    return pl.ds(pl.multiple_of(index * size, size), size)


def hop_kernel(ids, cols, table, tiles_hbm, out, rows, picked, tiles, sem):
    width = table.shape[0]
    blocks = tiles.shape[0]
    group = blocks // 8
    copies = [
        pltpu.make_async_copy(
            tiles_hbm.at[pl.ds(j * group, group)], tiles.at[pl.ds(j * group, group)], sem.at[j]
        )
        for j in range(8)
    ]
    for copy in copies:
        copy.start()

    def turn(b, carry):
        rows[aligned(b, TILE), 0:width] = table[:, aligned(b, TILE)].astype(F32).T
        return carry

    lax.fori_loop(0, table.shape[1] // TILE, turn, 0, unroll=8)
    step = 64

    def pick(g, carry):
        base = pl.multiple_of(g * step, step)
        for u in range(step):
            picked[pl.ds(base + u, 1), :] = rows[pl.ds(ids[base + u], 1), :]
        return carry

    lax.fori_loop(0, ids.shape[0] // step, pick, 0)
    for copy in copies:
        copy.wait()

    def merge(r, carry):
        out[r, 0:width, :] = picked[aligned(r, TILE), :].T[0:width].astype(BF)
        left = jnp.concatenate([tiles[r, k] for k in range(8)], axis=1)
        right = jnp.concatenate(
            [picked[aligned(cols[r * 8 + k], TILE), :].astype(BF) for k in range(8)], axis=0
        )
        total = jnp.dot(left, right, preferred_element_type=F32)
        out[r, width : 2 * width, :] = total.T[0:width].astype(BF)
        return carry

    lax.fori_loop(0, blocks, merge, 0, unroll=2)


def hop(table, ids, cols, tiles):
    blocks = tiles.shape[0]
    return pl.pallas_call(
        hop_kernel,
        in_specs=[SMEM, SMEM, VMEM, HBM],
        out_specs=VMEM,
        scratch_shapes=[
            pltpu.VMEM((table.shape[1], TILE), F32),
            pltpu.VMEM((ids.shape[0], TILE), F32),
            pltpu.VMEM(tiles.shape, BF),
            pltpu.SemaphoreType.DMA((8,)),
        ],
        out_shape=jax.ShapeDtypeStruct((blocks, 2 * table.shape[0], TILE), BF),
        compiler_params=LIMIT,
        cost_estimate=pl.CostEstimate(flops=10**9, bytes_accessed=60 * 10**6, transcendentals=0),
    )(ids, cols.reshape(-1), table, tiles)


def pack_kernel(place, own, neigh, bias, head_self, head_neigh, weights, heads):
    core, x, feat = place[0], place[1], place[2]
    cols = aligned(x, 256)
    chosen = jnp.where(core == 0, own[:, cols], neigh[:, cols]).astype(F32)
    lane = lax.broadcasted_iota(jnp.int32, (8, 256), 1) + x * 256
    row = lax.broadcasted_iota(jnp.int32, (8, 256), 0)
    left = jnp.concatenate([bias[...]] * 8, axis=1)
    high = left.astype(BF).astype(F32)
    left = left - high
    middle = left.astype(BF).astype(F32)
    low = left - middle
    term = jnp.where(row == 0, high, jnp.where(row == 1, middle, jnp.where(row == 2, low, 0.0)))
    inside = jnp.logical_and(lane >= feat * 32, lane < feat * 32 + 32)
    term = jnp.where(jnp.logical_and(inside, core == 0), term, 0.0)
    block = jnp.concatenate([chosen, term], axis=0).astype(BF)
    for d in range(weights.shape[0]):
        weights[d] = block
    classes = head_self.shape[1]
    heads[...] = jnp.zeros_like(heads)
    for d in range(heads.shape[0]):
        heads[d, 0:32, 0:classes] = head_self[...]
        heads[d, 32:64, 0:classes] = head_neigh[...]


def pack(place, own, neigh, bias, head_self, head_neigh):
    return pl.pallas_call(
        pack_kernel,
        in_specs=[SMEM] + [VMEM] * 5,
        out_specs=[VMEM, VMEM],
        out_shape=[
            jax.ShapeDtypeStruct((32, 32, 256), BF),
            jax.ShapeDtypeStruct((4, 64, 256), BF),
        ],
        compiler_params=LIMIT,
    )(place, own, neigh, bias.reshape(1, -1), head_self, head_neigh)


def spread_kernel(cols, live, logit_cot, heads, tiles, out, cot):
    classes, slots = logit_cot.shape
    lane = lax.broadcasted_iota(jnp.int32, (classes, slots), 1)
    kept = jnp.where(lane < live[0], logit_cot[...].astype(F32), 0.0)
    cot[...] = jnp.concatenate([kept, jnp.zeros((256 - classes, slots), F32)], axis=0).astype(BF)
    out[...] = jnp.zeros_like(out)
    own = jnp.concatenate([heads[j, 0:32] for j in range(4)], axis=0)
    neigh = jnp.concatenate([heads[j, 32:64] for j in range(4)], axis=0)
    for r in range(tiles.shape[0]):
        part = cot[:, r * TILE : (r + 1) * TILE]
        out[r] = jnp.dot(own, part, preferred_element_type=F32)
    for r in range(tiles.shape[0]):
        part = cot[:, r * TILE : (r + 1) * TILE]
        back = jnp.dot(neigh, part, preferred_element_type=F32).astype(BF)
        for k in range(8):
            out[cols[r * 8 + k]] += jnp.dot(back, tiles[r, k], preferred_element_type=F32)


def spread(cols, live, logit_cot, heads, tiles, blocks):
    return pl.pallas_call(
        spread_kernel,
        in_specs=[SMEM, SMEM, VMEM, VMEM, VMEM],
        out_specs=[VMEM, VMEM],
        out_shape=[
            jax.ShapeDtypeStruct((blocks, TILE, TILE), F32),
            jax.ShapeDtypeStruct((256, logit_cot.shape[1]), BF),
        ],
        compiler_params=LIMIT,
        cost_estimate=pl.CostEstimate(flops=10**9, bytes_accessed=8 * 10**6, transcendentals=0),
    )(cols.reshape(-1), live.reshape(1), logit_cot, heads, tiles)


def layer_kernel(place, got, w0, w1, w2, w3, o0, o1, o2, o3, out, mine, other):
    core, x = place[0], place[1]
    deep = got.shape[1] // 2
    row = lax.broadcasted_iota(jnp.int32, (8, TILE), 0)
    ones = jnp.where(row < 3, 1.0, 0.0)

    for j in range(8):
        own, agg = [], []
        for i in range(4):
            piece = got[4 * j + i].astype(F32)
            own += [piece[0:deep], ones]
            agg += [piece[deep : 2 * deep], ones]
        own = jnp.concatenate(own, axis=0).T.astype(BF)
        agg = jnp.concatenate(agg, axis=0).T.astype(BF)
        at = slice(j * TILE, (j + 1) * TILE)
        mine[:, at] = jnp.where(core == 0, own, agg)
        other[:, at] = jnp.where(core == 0, agg, own)
    for s, (w, o) in enumerate(((w0, o0), (w1, o1), (w2, o2), (w3, o3))):
        chunk = lax.rem(x + 4 - s, 4)
        preact = jnp.dot(mine[...], w[...], preferred_element_type=F32)
        preact = preact + jnp.dot(other[...], o[...], preferred_element_type=F32)
        hidden = jnp.maximum(preact, 0.0)
        for half in range(2):
            piece = hidden[:, half * TILE : (half + 1) * TILE].T.astype(BF)
            for y in range(4):
                out[(2 * chunk + half) * 4 + y] = piece


def layer(place, got, mine, other):
    return pl.pallas_call(
        layer_kernel,
        in_specs=[SMEM] + [VMEM] * 9,
        out_specs=VMEM,
        scratch_shapes=[pltpu.VMEM((TILE, 1024), BF), pltpu.VMEM((TILE, 1024), BF)],
        out_shape=jax.ShapeDtypeStruct((32, TILE, TILE), BF),
        compiler_params=LIMIT,
    )(place, got, *mine, *other)


def score_kernel(place, cols, hidden, dhidden, tiles, cot, pair, out, heads, second):
    y = place[3]
    own = pl.ds(pl.multiple_of(y * 32, 32), 32)
    for r in range(tiles.shape[0]):
        left = jnp.concatenate([hidden[cols[r * 8 + k]] for k in range(8)], axis=1)
        right = jnp.concatenate([tiles[r, k] for k in range(8)], axis=1)
        second[r] = lax.dot_general(left, right, NT, preferred_element_type=F32).astype(BF)
    self_t = jnp.concatenate([pair[j, 0:32] for j in range(4)], axis=0).astype(F32).T.astype(BF)
    neigh_t = jnp.concatenate([pair[j, 32:64] for j in range(4)], axis=0).astype(F32).T.astype(BF)
    for half in range(2):
        at = 2 * y + half
        scores = jnp.dot(self_t, hidden[at], preferred_element_type=F32)
        scores = scores + jnp.dot(neigh_t, second[at], preferred_element_type=F32)
        for z in range(out.shape[0]):
            out[z, 32 * half : 32 * half + 24, :] = scores[24 * z : 24 * (z + 1)].astype(BF)
    total = jnp.zeros((32, TILE), F32)
    for b in range(hidden.shape[0]):
        total = total + jnp.where(hidden[b, own, :].astype(F32) > 0.0, dhidden[b, own, :], 0.0)
    mine = jnp.sum(total, axis=1, keepdims=True)
    targets = jnp.concatenate([hidden[r, own, :] for r in range(tiles.shape[0])], axis=1)
    merged = jnp.concatenate([second[r, own, :] for r in range(tiles.shape[0])], axis=1)
    lane = lax.broadcasted_iota(jnp.int32, (32, 256), 1)
    grad = lax.dot_general(targets, cot[...], NT, preferred_element_type=F32)
    heads[:, 0:256] = jnp.where(lane == 255, mine, grad)
    heads[:, 256:512] = lax.dot_general(merged, cot[...], NT, preferred_element_type=F32)


def score(place, cols, hidden, dhidden, tiles, cot, pair):
    return pl.pallas_call(
        score_kernel,
        in_specs=[SMEM, SMEM] + [VMEM] * 5,
        out_specs=[VMEM, VMEM],
        scratch_shapes=[pltpu.VMEM((tiles.shape[0], TILE, TILE), BF)],
        out_shape=[
            jax.ShapeDtypeStruct((8, 64, TILE), BF),
            jax.ShapeDtypeStruct((32, 512), F32),
        ],
        compiler_params=LIMIT,
    )(place, cols.reshape(-1), hidden, dhidden, tiles, cot, pair)


def grad_kernel(place, hidden, dhidden, feats, keep, send, total):
    core = place[0]
    groups, blocks, deep, _ = feats.shape
    half = deep // 2
    total[...] = jnp.zeros_like(total)

    def grow(b, carry):
        low = jnp.where(hidden[b].astype(F32) > 0.0, dhidden[b], 0.0).astype(BF)
        stack = jnp.concatenate([feats[z, b] for z in range(groups)], axis=0)
        total[...] += lax.dot_general(stack, low, NT, preferred_element_type=F32)
        return carry

    lax.fori_loop(0, blocks, grow, 0, unroll=4)
    for z in range(groups):
        keep[z] = total[pl.ds(pl.multiple_of(z * deep + core * half, 8), half), :]
        send[z] = total[pl.ds(pl.multiple_of(z * deep + (1 - core) * half, 8), half), :]


def grad(place, hidden, dhidden, feats):
    groups, blocks, deep, _ = feats.shape
    shape = jax.ShapeDtypeStruct((groups, deep // 2, TILE), F32)
    return pl.pallas_call(
        grad_kernel,
        in_specs=[SMEM] + [VMEM] * 3,
        out_specs=[VMEM, VMEM],
        scratch_shapes=[pltpu.VMEM((groups * deep, TILE), F32)],
        out_shape=[shape, shape],
        compiler_params=LIMIT,
        cost_estimate=pl.CostEstimate(flops=10**9, bytes_accessed=7 * 10**6, transcendentals=0),
    )(place, hidden, dhidden, feats)


def swap_core(value):
    return lax.ppermute(value, "core", [(0, 1), (1, 0)])


def sum_x(value):
    value = value + lax.ppermute(value, "x", [(0, 1), (1, 0), (2, 3), (3, 2)])
    return value + lax.ppermute(value, "x", [(0, 3), (3, 0), (1, 2), (2, 1)])


def shards(
    feature_table,
    node_ids,
    hop_cols,
    hop_tiles,
    target_cols,
    target_tiles,
    self_weight,
    neigh_weight,
    hidden_bias,
    head_self,
    head_neigh,
    batch_sizes,
    logit_cotangent,
):
    blocks = hop_cols.shape[0]
    classes, target_rows = logit_cotangent.shape
    x, core = lax.axis_index("x"), lax.axis_index("core")
    y = lax.axis_index("y")
    place = jnp.stack([core, x, lax.axis_index("z") * 4 + y, y])

    weights, pair = pack(place, self_weight, neigh_weight, hidden_bias, head_self, head_neigh)
    weights = lax.all_to_all(weights, FEAT, 0, 0, tiled=True).reshape(1024, 256)
    mine = [weights] + [
        lax.ppermute(weights, "x", [(i, (i + s) % 4) for i in range(4)]) for s in (1, 2, 3)
    ]
    other = [swap_core(w) for w in mine]
    pair = lax.all_to_all(pair, "y", 0, 0, tiled=True)

    live = batch_sizes[x * 2 + core]
    dhidden, cot = spread(target_cols, live, logit_cotangent, pair, target_tiles, blocks)

    send = hop(feature_table, node_ids, hop_cols, hop_tiles)
    feats = lax.all_gather(send, "z", axis=0, tiled=False)
    got = lax.all_to_all(send, FEAT, 0, 0, tiled=True)
    hidden = layer(place, got, mine, other)
    hidden = lax.all_to_all(hidden, FEAT, 0, 0, tiled=True)

    scores, heads = score(place, target_cols, hidden, dhidden, target_tiles, cot, pair)
    scores = lax.all_to_all(scores, "z", 0, 0, tiled=True)
    scores = jnp.sum(scores.astype(F32), axis=0).astype(BF)
    scores = lax.all_to_all(
        jnp.broadcast_to(scores[None], (32,) + scores.shape), FEAT, 0, 0, tiled=True
    )
    scores = scores.reshape(8, 4, 2, 32, TILE)[:, :, :, :24].transpose(0, 3, 1, 2, 4)
    logits = scores.reshape(192, target_rows)[:classes].astype(F32)

    heads = sum_x(heads + swap_core(heads))
    keep, send = grad(place, hidden, dhidden, feats)
    keep = keep + swap_core(send)
    keep = sum_x(lax.all_to_all(keep, "z", 0, 0, tiled=True))
    keep = keep.transpose(1, 0, 2).reshape(-1, 1024)
    rest = swap_core(keep)
    return (
        logits,
        jnp.where(core == 0, keep, rest),
        jnp.where(core == 0, rest, keep),
        heads[:, :classes],
        heads[:, 256 : 256 + classes],
        heads[:, 255],
    )


def solution(mesh):
    split = Mesh(mesh.devices.reshape(4, 2, 8, 4), DP + FEAT)
    return jax.shard_map(
        shards,
        mesh=split,
        in_specs=(
            P(FEAT, None),
            P(DP),
            P(DP, None),
            P(DP, None, None, None),
            P(DP, None),
            P(DP, None, None, None),
            P(FEAT, None),
            P(FEAT, None),
            P(FEAT),
            P(FEAT, None),
            P(FEAT, None),
            P(),
            P(None, DP),
        ),
        out_specs=(
            P(None, DP),
            P(FEAT, None),
            P(FEAT, None),
            P(FEAT, None),
            P(FEAT, None),
            P(FEAT),
        ),
        check_vma=False,
    )
```

```python
import jax
import jax.numpy as jnp
from jax import lax
from jax.experimental import pallas as pl
from jax.experimental.pallas import tpu as pltpu
from jax.sharding import Mesh, PartitionSpec as P

TILE = 128
FEAT = ("z", "y")
DP = ("x", "core")
BF = jnp.bfloat16
F32 = jnp.float32
NT = (((1,), (1,)), ((), ()))
VMEM = pl.BlockSpec(memory_space=pltpu.VMEM)
SMEM = pl.BlockSpec(memory_space=pltpu.SMEM)
HBM = pl.BlockSpec(memory_space=pl.ANY)
LIMIT = pltpu.CompilerParams(vmem_limit_bytes=56 * 2**20)


def aligned(index, size):
    return pl.ds(pl.multiple_of(index * size, size), size)


def hop_kernel(place, ids, cols, table, bias, tiles_hbm, _, out, feats, rows, picked, tiles, sem):
    width = table.shape[0]
    blocks = tiles.shape[0]
    group = blocks // 8
    copies = [
        pltpu.make_async_copy(
            tiles_hbm.at[pl.ds(j * group, group)], tiles.at[pl.ds(j * group, group)], sem.at[j]
        )
        for j in range(8)
    ]
    for copy in copies:
        copy.start()

    def turn(b, carry):
        rows[aligned(b, TILE), 0:width] = table[:, aligned(b, TILE)].astype(F32).T
        return carry

    lax.fori_loop(0, table.shape[1] // TILE, turn, 0, unroll=8)
    step = 64
    lane = lax.broadcasted_iota(jnp.int32, (8, TILE), 1)
    row = lax.broadcasted_iota(jnp.int32, (8, TILE), 0)
    left = jnp.concatenate([bias[...]] * 4, axis=1)
    high = left.astype(BF).astype(F32)
    left = left - high
    middle = left.astype(BF).astype(F32)
    low = left - middle
    term = jnp.where(row == 0, high, jnp.where(row == 1, middle, jnp.where(row == 2, low, 0.0)))
    term = jnp.where(lane // 32 == place[3], term, 0.0).astype(BF)

    def pick(g, carry):
        base = pl.multiple_of(g * step, step)
        for u in range(step):
            picked[pl.ds(base + u, 1), :] = rows[pl.ds(ids[base + u], 1), :]
        return carry

    lax.fori_loop(0, ids.shape[0] // step, pick, 0)
    for copy in copies:
        copy.wait()

    def merge(r, carry):
        own = picked[aligned(r, TILE), :].T[0:width]
        left = jnp.concatenate([tiles[r, k] for k in range(8)], axis=1)
        right = jnp.concatenate(
            [picked[aligned(cols[r * 8 + k], TILE), :].astype(BF) for k in range(8)], axis=0
        )
        total = jnp.dot(left, right, preferred_element_type=F32)
        both = jnp.concatenate([own, total.T[0:width]], axis=0).astype(BF)
        out[r, 0 : 2 * width, :] = both
        feats[r] = both
        out[r, 2 * width :, :] = term
        return carry

    lax.fori_loop(0, blocks, merge, 0, unroll=2)


def hop(place, table, ids, cols, bias, tiles, after):
    blocks, deep = tiles.shape[0], 2 * table.shape[0]
    return pl.pallas_call(
        hop_kernel,
        in_specs=[SMEM, SMEM, SMEM, VMEM, VMEM, HBM, HBM],
        out_specs=[VMEM, VMEM],
        scratch_shapes=[
            pltpu.VMEM((table.shape[1], TILE), F32),
            pltpu.VMEM((ids.shape[0], TILE), F32),
            pltpu.VMEM(tiles.shape, BF),
            pltpu.SemaphoreType.DMA((8,)),
        ],
        out_shape=[
            jax.ShapeDtypeStruct((blocks, deep + 8, TILE), BF),
            jax.ShapeDtypeStruct((blocks, deep, TILE), BF),
        ],
        compiler_params=LIMIT,
        cost_estimate=pl.CostEstimate(flops=10**9, bytes_accessed=60 * 10**6, transcendentals=0),
    )(place, ids, cols.reshape(-1), table, bias.reshape(1, -1), tiles, after)


def pack_kernel(place, own, neigh, head_self, head_neigh, weights, heads):
    core, x = place[0], place[1]
    cols = aligned(x, 256)
    block = jnp.where(core == 0, own[:, cols].astype(F32), neigh[:, cols].astype(F32)).astype(BF)
    for d in range(weights.shape[0]):
        weights[d] = block
    classes = head_self.shape[1]
    heads[...] = jnp.zeros_like(heads)
    for d in range(heads.shape[0]):
        heads[d, 0:32, 0:classes] = head_self[...]
        heads[d, 32:64, 0:classes] = head_neigh[...]


def pack(place, own, neigh, head_self, head_neigh):
    return pl.pallas_call(
        pack_kernel,
        in_specs=[SMEM] + [VMEM] * 4,
        out_specs=[VMEM, VMEM],
        out_shape=[
            jax.ShapeDtypeStruct((32, own.shape[0], 256), BF),
            jax.ShapeDtypeStruct((4, 64, 256), BF),
        ],
        compiler_params=LIMIT,
    )(place, own, neigh, head_self, head_neigh)


def spread_kernel(cols, live, logit_cot, heads, tiles, out, cot):
    classes, slots = logit_cot.shape
    lane = lax.broadcasted_iota(jnp.int32, (classes, slots), 1)
    kept = jnp.where(lane < live[0], logit_cot[...].astype(F32), 0.0)
    cot[...] = jnp.concatenate([kept, jnp.zeros((256 - classes, slots), F32)], axis=0).astype(BF)
    out[...] = jnp.zeros_like(out)
    own = jnp.concatenate([heads[j, 0:32] for j in range(4)], axis=0)
    neigh = jnp.concatenate([heads[j, 32:64] for j in range(4)], axis=0)
    for r in range(tiles.shape[0]):
        part = cot[:, r * TILE : (r + 1) * TILE]
        out[r] = jnp.dot(own, part, preferred_element_type=F32)
    for r in range(tiles.shape[0]):
        part = cot[:, r * TILE : (r + 1) * TILE]
        back = jnp.dot(neigh, part, preferred_element_type=F32).astype(BF)
        for k in range(8):
            out[cols[r * 8 + k]] += jnp.dot(back, tiles[r, k], preferred_element_type=F32)


def spread(cols, live, logit_cot, heads, tiles, blocks):
    return pl.pallas_call(
        spread_kernel,
        in_specs=[SMEM, SMEM, VMEM, VMEM, VMEM],
        out_specs=[VMEM, VMEM],
        out_shape=[
            jax.ShapeDtypeStruct((blocks, TILE, TILE), F32),
            jax.ShapeDtypeStruct((256, logit_cot.shape[1]), BF),
        ],
        compiler_params=LIMIT,
        cost_estimate=pl.CostEstimate(flops=10**9, bytes_accessed=8 * 10**6, transcendentals=0),
    )(cols.reshape(-1), live.reshape(1), logit_cot, heads, tiles)


def layer_kernel(place, got, w0, w1, w2, w3, o0, o1, o2, o3, out, mine, other):
    core, x = place[0], place[1]
    deep = w0.shape[0] // 32
    for j in range(8):
        pieces = [got[4 * j + i, 0 : 2 * deep, :].astype(F32) for i in range(4)]
        own = jnp.concatenate([piece[0:deep] for piece in pieces], axis=0).T.astype(BF)
        agg = jnp.concatenate([piece[deep:] for piece in pieces], axis=0).T.astype(BF)
        at = slice(j * 4 * deep, (j + 1) * 4 * deep)
        mine[:, at] = jnp.where(core == 0, own, agg)
        other[:, at] = jnp.where(core == 0, agg, own)
    for s, (w, o) in enumerate(((w0, o0), (w1, o1), (w2, o2), (w3, o3))):
        chunk = lax.rem(x + 4 - s, 4)
        preact = jnp.dot(mine[...], w[...], preferred_element_type=F32)
        preact = preact + jnp.dot(other[...], o[...], preferred_element_type=F32)
        for half in range(2):
            z = 2 * chunk + half
            terms = sum(got[4 * z + i, 2 * deep : 2 * deep + 8, :].astype(F32) for i in range(4))
            bias = jnp.sum(terms, axis=0, keepdims=True)
            hidden = jnp.maximum(preact[:, half * TILE : (half + 1) * TILE] + bias, 0.0)
            out[z] = hidden.T.astype(BF)


def layer(place, got, mine, other):
    return pl.pallas_call(
        layer_kernel,
        in_specs=[SMEM] + [VMEM] * 9,
        out_specs=VMEM,
        scratch_shapes=[pltpu.VMEM((TILE, mine[0].shape[0]), BF)] * 2,
        out_shape=jax.ShapeDtypeStruct((8, TILE, TILE), BF),
        compiler_params=LIMIT,
    )(place, got, *mine, *other)


def score_kernel(
    place, cols, h0, h1, h2, h3, dhidden, tiles, cot, pair, out, heads, second, hidden
):
    y = place[3]
    for s, part in enumerate((h0, h1, h2, h3)):
        for z in range(part.shape[0]):
            hidden[4 * z + lax.rem(y + 4 - s, 4)] = part[z]
    own = pl.ds(pl.multiple_of(y * 32, 32), 32)
    for r in range(tiles.shape[0]):
        left = jnp.concatenate([hidden[cols[r * 8 + k]] for k in range(8)], axis=1)
        right = jnp.concatenate([tiles[r, k] for k in range(8)], axis=1)
        second[r] = lax.dot_general(left, right, NT, preferred_element_type=F32).astype(BF)
    self_t = jnp.concatenate([pair[j, 0:32] for j in range(4)], axis=0).astype(F32).T.astype(BF)
    neigh_t = jnp.concatenate([pair[j, 32:64] for j in range(4)], axis=0).astype(F32).T.astype(BF)
    for half in range(2):
        at = 2 * y + half
        scores = jnp.dot(self_t, hidden[at], preferred_element_type=F32)
        scores = scores + jnp.dot(neigh_t, second[at], preferred_element_type=F32)
        for z in range(out.shape[0]):
            out[z, 32 * half : 32 * half + 24, :] = scores[24 * z : 24 * (z + 1)].astype(BF)
    total = jnp.zeros((32, TILE), F32)
    for b in range(hidden.shape[0]):
        total = total + jnp.where(hidden[b, own, :].astype(F32) > 0.0, dhidden[b, own, :], 0.0)
    mine = jnp.sum(total, axis=1, keepdims=True)
    targets = jnp.concatenate([hidden[r, own, :] for r in range(tiles.shape[0])], axis=1)
    merged = jnp.concatenate([second[r, own, :] for r in range(tiles.shape[0])], axis=1)
    lane = lax.broadcasted_iota(jnp.int32, (32, 256), 1)
    grad = lax.dot_general(targets, cot[...], NT, preferred_element_type=F32)
    heads[:, 0:256] = jnp.where(lane == 255, mine, grad)
    heads[:, 256:512] = lax.dot_general(merged, cot[...], NT, preferred_element_type=F32)


def score(place, cols, hidden, dhidden, tiles, cot, pair):
    return pl.pallas_call(
        score_kernel,
        in_specs=[SMEM, SMEM] + [VMEM] * 8,
        out_specs=[VMEM, VMEM],
        scratch_shapes=[
            pltpu.VMEM((tiles.shape[0], TILE, TILE), BF),
            pltpu.VMEM((32, TILE, TILE), BF),
        ],
        out_shape=[
            jax.ShapeDtypeStruct((8, 64, TILE), BF),
            jax.ShapeDtypeStruct((32, 512), F32),
        ],
        compiler_params=LIMIT,
    )(place, cols.reshape(-1), *hidden, dhidden, tiles, cot, pair)


def grad_kernel(place, h0, h1, h2, h3, dhidden, feats, keep, send, total):
    core, y = place[0], place[3]
    groups, blocks, deep, _ = feats.shape
    half = deep // 2
    total[...] = jnp.zeros_like(total)
    for s, part in enumerate((h0, h1, h2, h3)):
        first = lax.rem(y + 4 - s, 4)

        def grow(z, carry):
            b = 4 * z + first
            low = jnp.where(part[z].astype(F32) > 0.0, dhidden[b], 0.0).astype(BF)
            stack = jnp.concatenate([feats[g, b] for g in range(groups)], axis=0)
            total[...] += lax.dot_general(stack, low, NT, preferred_element_type=F32)
            return carry

        lax.fori_loop(0, part.shape[0], grow, 0, unroll=4)
    for z in range(groups):
        keep[z] = total[pl.ds(pl.multiple_of(z * deep + core * half, 8), half), :]
        send[z] = total[pl.ds(pl.multiple_of(z * deep + (1 - core) * half, 8), half), :]


def grad(place, hidden, dhidden, feats):
    groups, blocks, deep, _ = feats.shape
    shape = jax.ShapeDtypeStruct((groups, deep // 2, TILE), F32)
    return pl.pallas_call(
        grad_kernel,
        in_specs=[SMEM] + [VMEM] * 6,
        out_specs=[VMEM, VMEM],
        scratch_shapes=[pltpu.VMEM((groups * deep, TILE), F32)],
        out_shape=[shape, shape],
        compiler_params=LIMIT,
        cost_estimate=pl.CostEstimate(flops=10**9, bytes_accessed=7 * 10**6, transcendentals=0),
    )(place, *hidden, dhidden, feats)


def shift(value, axis, by):
    return lax.ppermute(value, axis, [(i, (i + by) % 4) for i in range(4)])


def swap_core(value):
    return lax.ppermute(value, "core", [(0, 1), (1, 0)])


def sum_x(value):
    value = value + lax.ppermute(value, "x", [(0, 1), (1, 0), (2, 3), (3, 2)])
    return value + lax.ppermute(value, "x", [(0, 3), (3, 0), (1, 2), (2, 1)])


def shards(
    feature_table,
    node_ids,
    hop_cols,
    hop_tiles,
    target_cols,
    target_tiles,
    self_weight,
    neigh_weight,
    hidden_bias,
    head_self,
    head_neigh,
    batch_sizes,
    logit_cotangent,
):
    blocks = hop_cols.shape[0]
    classes, target_rows = logit_cotangent.shape
    x, core = lax.axis_index("x"), lax.axis_index("core")
    y = lax.axis_index("y")
    place = jnp.stack([core, x, lax.axis_index("z") * 4 + y, y])

    packed, pair = pack(place, self_weight, neigh_weight, head_self, head_neigh)
    weights = lax.all_to_all(packed, FEAT, 0, 0, tiled=True)
    pair = lax.all_to_all(pair, "y", 0, 0, tiled=True)

    send, feats = hop(
        place, feature_table, node_ids, hop_cols, hidden_bias, hop_tiles, packed
    )
    weights, pair, send, feats = lax.optimization_barrier((weights, pair, send, feats))
    got = lax.all_to_all(send, FEAT, 0, 0, tiled=True)
    feats = lax.all_gather(feats, "z", axis=0, tiled=False)
    weights = weights.reshape(-1, 256)
    mine = [weights] + [shift(weights, "x", s) for s in (1, 2, 3)]
    other = [swap_core(w) for w in mine]

    live = batch_sizes[x * 2 + core]
    dhidden, cot = spread(target_cols, live, logit_cotangent, pair, target_tiles, blocks)

    hidden = layer(place, got, mine, other)
    hidden = lax.all_to_all(hidden, "z", 0, 0, tiled=True)
    hidden = [hidden] + [shift(hidden, "y", s) for s in (1, 2, 3)]

    scores, heads = score(place, target_cols, hidden, dhidden, target_tiles, cot, pair)
    scores = lax.all_to_all(scores, "z", 0, 0, tiled=True)
    keep, send = grad(place, hidden, dhidden, feats)
    scores = jnp.sum(scores.astype(F32), axis=0).astype(BF)
    scores = lax.all_to_all(
        jnp.broadcast_to(scores[None], (32,) + scores.shape), FEAT, 0, 0, tiled=True
    )
    scores = scores.reshape(8, 4, 2, 32, TILE)[:, :, :, :24].transpose(0, 3, 1, 2, 4)
    logits = scores.reshape(192, target_rows)[:classes].astype(F32)

    keep = keep + swap_core(send)
    keep = lax.all_to_all(keep, "z", 0, 0, tiled=True)
    heads = heads + swap_core(heads)
    joined = sum_x(jnp.concatenate([keep.reshape(-1, TILE), heads.reshape(-1, TILE)], axis=0))
    heads = joined[keep.size // TILE :].reshape(heads.shape)
    keep = joined[: keep.size // TILE].reshape(keep.shape).transpose(1, 0, 2).reshape(-1, 1024)
    rest = swap_core(keep)
    return (
        logits,
        jnp.where(core == 0, keep, rest),
        jnp.where(core == 0, rest, keep),
        heads[:, :classes],
        heads[:, 256 : 256 + classes],
        heads[:, 255],
    )


def solution(mesh):
    split = Mesh(mesh.devices.reshape(4, 2, 8, 4), DP + FEAT)
    return jax.shard_map(
        shards,
        mesh=split,
        in_specs=(
            P(FEAT, None),
            P(DP),
            P(DP, None),
            P(DP, None, None, None),
            P(DP, None),
            P(DP, None, None, None),
            P(FEAT, None),
            P(FEAT, None),
            P(FEAT),
            P(FEAT, None),
            P(FEAT, None),
            P(),
            P(None, DP),
        ),
        out_specs=(
            P(None, DP),
            P(FEAT, None),
            P(FEAT, None),
            P(FEAT, None),
            P(FEAT, None),
            P(FEAT),
        ),
        check_vma=False,
    )
```

```python
import jax
import jax.numpy as jnp
from jax import lax
from jax.experimental import pallas as pl
from jax.experimental.pallas import tpu as pltpu
from jax.sharding import Mesh, PartitionSpec as P

TILE = 128
FEAT = ("zq", "zr", "y")
DP = ("x", "core")
BF = jnp.bfloat16
F32 = jnp.float32
NT = (((1,), (1,)), ((), ()))
VMEM = pl.BlockSpec(memory_space=pltpu.VMEM)
SMEM = pl.BlockSpec(memory_space=pltpu.SMEM)
HBM = pl.BlockSpec(memory_space=pl.ANY)
LIMIT = pltpu.CompilerParams(vmem_limit_bytes=56 * 2**20)


def aligned(index, size):
    return pl.ds(pl.multiple_of(index * size, size), size)


def split_bias(bias):
    row = lax.broadcasted_iota(jnp.int32, (8, bias.shape[1]), 0)
    left = jnp.broadcast_to(bias, row.shape)
    high = left.astype(BF).astype(F32)
    left = left - high
    middle = left.astype(BF).astype(F32)
    low = left - middle
    return jnp.where(row == 0, high, jnp.where(row == 1, middle, jnp.where(row == 2, low, 0.0)))


def hop_kernel(place, ids, cols, table, bias, tiles_hbm, _, out, feats, rows, picked, tiles, sem):
    width = table.shape[0]
    blocks = tiles.shape[0]
    group = blocks // 8
    copies = [
        pltpu.make_async_copy(
            tiles_hbm.at[pl.ds(j * group, group)], tiles.at[pl.ds(j * group, group)], sem.at[j]
        )
        for j in range(8)
    ]
    for copy in copies:
        copy.start()

    def turn(b, carry):
        rows[aligned(b, TILE), 0:width] = table[:, aligned(b, TILE)].astype(F32).T
        return carry

    lax.fori_loop(0, table.shape[1] // TILE, turn, 0, unroll=8)
    step = 64

    def pick(g, carry):
        base = pl.multiple_of(g * step, step)
        for u in range(step):
            picked[pl.ds(base + u, 1), :] = rows[pl.ds(ids[base + u], 1), :]
        return carry

    lax.fori_loop(0, ids.shape[0] // step, pick, 0)
    lane = lax.broadcasted_iota(jnp.int32, (8, TILE), 1)
    term = split_bias(jnp.concatenate([bias[...]] * 4, axis=1))
    term = jnp.where(lane // 32 == place[4], term, 0.0)
    for copy in copies:
        copy.wait()

    def merge(r, carry):
        own = picked[aligned(r, TILE), :].T[0:width]
        left = jnp.concatenate([tiles[r, k] for k in range(8)], axis=1)
        right = jnp.concatenate(
            [picked[aligned(cols[r, k], TILE), :].astype(BF) for k in range(8)], axis=0
        )
        total = jnp.dot(left, right, preferred_element_type=F32)
        both = jnp.concatenate([own, total.T[0:width]], axis=0)
        feats[r] = both.astype(BF)
        out[r] = jnp.concatenate([both, term], axis=0).astype(BF)
        return carry

    lax.fori_loop(0, blocks, merge, 0, unroll=2)


def hop(place, table, ids, cols, bias, tiles, after):
    blocks, deep = tiles.shape[0], 2 * table.shape[0]
    return pl.pallas_call(
        hop_kernel,
        in_specs=[SMEM, SMEM, SMEM, VMEM, VMEM, HBM, HBM],
        out_specs=[VMEM, VMEM],
        scratch_shapes=[
            pltpu.VMEM((table.shape[1], TILE), F32),
            pltpu.VMEM((ids.shape[0], TILE), F32),
            pltpu.VMEM(tiles.shape, BF),
            pltpu.SemaphoreType.DMA((8,)),
        ],
        out_shape=[
            jax.ShapeDtypeStruct((blocks, deep + 8, TILE), BF),
            jax.ShapeDtypeStruct((blocks, deep, TILE), BF),
        ],
        compiler_params=LIMIT,
        cost_estimate=pl.CostEstimate(flops=10**9, bytes_accessed=60 * 10**6, transcendentals=0),
    )(place, ids, cols, table, bias.reshape(1, -1), tiles, after)


def pack_kernel(place, own, neigh, head_self, head_neigh, weights, heads):
    core, x = place[0], place[1]
    cols = aligned(lax.rem(x, 2), 512)
    block = jnp.where(core == 0, own[:, cols].astype(F32), neigh[:, cols].astype(F32)).astype(BF)
    for d in range(weights.shape[0]):
        weights[d] = block
    classes = head_self.shape[1]
    heads[...] = jnp.zeros_like(heads)
    heads[0:32, 0:classes] = head_self[...]
    heads[32:64, 0:classes] = head_neigh[...]


def pack(place, own, neigh, head_self, head_neigh):
    return pl.pallas_call(
        pack_kernel,
        in_specs=[SMEM] + [VMEM] * 4,
        out_specs=[VMEM, VMEM],
        out_shape=[
            jax.ShapeDtypeStruct((32, own.shape[0], 512), BF),
            jax.ShapeDtypeStruct((64, 256), BF),
        ],
        compiler_params=LIMIT,
    )(place, own, neigh, head_self, head_neigh)


def spread_kernel(
    place, cols, live, logit_cot, p0, p1, p2, p3, tiles, out, cot, self_t, neigh_t, own, neigh
):
    classes, slots = logit_cot.shape
    lane = lax.broadcasted_iota(jnp.int32, (classes, slots), 1)
    kept = jnp.where(lane < live[0], logit_cot[...].astype(F32), 0.0)
    cot[...] = jnp.concatenate([kept, jnp.zeros((256 - classes, slots), F32)], axis=0).astype(BF)
    out[...] = jnp.zeros_like(out)
    for s, part in enumerate((p0, p1, p2, p3)):
        at = aligned(lax.rem(place[2] + 4 - s, 4), 32)
        own[at, :] = part[0:32]
        neigh[at, :] = part[32:64]
    self_t[...] = own[...].astype(F32).T.astype(BF)
    neigh_t[...] = neigh[...].astype(F32).T.astype(BF)
    for r in range(tiles.shape[0]):
        part = cot[:, r * TILE : (r + 1) * TILE]
        out[r] = jnp.dot(own[...], part, preferred_element_type=F32)
    for r in range(tiles.shape[0]):
        part = cot[:, r * TILE : (r + 1) * TILE]
        back = jnp.dot(neigh[...], part, preferred_element_type=F32).astype(BF)
        for k in range(8):
            out[cols[r, k]] += jnp.dot(back, tiles[r, k], preferred_element_type=F32)


def spread(place, cols, live, logit_cot, pairs, tiles, blocks):
    return pl.pallas_call(
        spread_kernel,
        in_specs=[SMEM, SMEM, SMEM] + [VMEM] * 6,
        out_specs=[VMEM] * 4,
        scratch_shapes=[pltpu.VMEM((TILE, 256), BF)] * 2,
        out_shape=[
            jax.ShapeDtypeStruct((blocks, TILE, TILE), F32),
            jax.ShapeDtypeStruct((256, logit_cot.shape[1]), BF),
            jax.ShapeDtypeStruct((256, TILE), BF),
            jax.ShapeDtypeStruct((256, TILE), BF),
        ],
        compiler_params=LIMIT,
        cost_estimate=pl.CostEstimate(flops=10**9, bytes_accessed=8 * 10**6, transcendentals=0),
    )(place, cols, live.reshape(1), logit_cot, *pairs, tiles)


def layer_kernel(place, got, w0, w1, w2, o0, o1, o2, out, mine, other):
    core, x = place[0], place[1]
    deep = w0.shape[0] // 32
    for j in range(8):
        pieces = [got[4 * j + i].astype(F32) for i in range(4)]
        own = jnp.concatenate([piece[0:deep] for piece in pieces], axis=0).T.astype(BF)
        agg = jnp.concatenate([piece[deep : 2 * deep] for piece in pieces], axis=0).T.astype(BF)
        at = slice(j * 4 * deep, (j + 1) * 4 * deep)
        mine[:, at] = jnp.where(core == 0, own, agg)
        other[:, at] = jnp.where(core == 0, agg, own)

    def emit(chunk, w, o):
        preact = jnp.dot(mine[...], w, preferred_element_type=F32)
        preact = preact + jnp.dot(other[...], o, preferred_element_type=F32)
        rows = aligned(chunk, 32)
        for half in range(2):
            z = 2 * chunk + half
            terms = sum(got[4 * z + i].astype(F32)[2 * deep :] for i in range(4))
            bias = jnp.sum(terms, axis=0, keepdims=True)
            hidden = jnp.maximum(preact[:, half * TILE : (half + 1) * TILE] + bias, 0.0)
            hidden = hidden.T.astype(BF)
            for y in range(4):
                for zq in range(4):
                    out[8 * zq + 4 * half + y, rows, :] = hidden[32 * y : 32 * y + 32]

    near = 2 * lax.rem(x, 2)
    far = 2 - near
    emit(near, w0[:, 0:256], o0[:, 0:256])
    emit(near + 1, w0[:, 256:512], o0[:, 256:512])
    emit(far, w1[...], o1[...])
    emit(far + 1, w2[...], o2[...])


def layer(place, got, mine, other):
    return pl.pallas_call(
        layer_kernel,
        in_specs=[SMEM] + [VMEM] * 7,
        out_specs=VMEM,
        scratch_shapes=[pltpu.VMEM((TILE, mine[0].shape[0]), BF)] * 2,
        out_shape=jax.ShapeDtypeStruct((32, TILE, TILE), BF),
        compiler_params=LIMIT,
    )(place, got, *mine, *other)


def score_kernel(
    place, cols, hidden, dhidden, tiles, cot, self_t, neigh_t, out, keep, send, second
):
    core, zq = place[0], place[2]
    own = aligned(zq, 32)
    for r in range(tiles.shape[0]):
        left = jnp.concatenate([hidden[cols[r, k]] for k in range(8)], axis=1)
        right = jnp.concatenate([tiles[r, k] for k in range(8)], axis=1)
        second[r] = lax.dot_general(left, right, NT, preferred_element_type=F32).astype(BF)
    halves = []
    for half in range(2):
        at = 2 * zq + half
        scores = jnp.dot(self_t[...], hidden[at], preferred_element_type=F32)
        halves.append(scores + jnp.dot(neigh_t[...], second[at], preferred_element_type=F32))
    for z in range(out.shape[0]):
        both = [scores[24 * z : 24 * (z + 1)] for scores in halves]
        out[z] = jnp.concatenate(both, axis=0).astype(BF)
    total = jnp.zeros((32, TILE), F32)
    for b in range(hidden.shape[0]):
        total = total + jnp.where(hidden[b, own, :].astype(F32) > 0.0, dhidden[b, own, :], 0.0)
    mine = jnp.sum(total, axis=1, keepdims=True)
    targets = jnp.concatenate([hidden[r, own, :] for r in range(tiles.shape[0])], axis=1)
    merged = jnp.concatenate([second[r, own, :] for r in range(tiles.shape[0])], axis=1)
    lane = lax.broadcasted_iota(jnp.int32, (32, 256), 1)
    first = lax.dot_general(targets, cot[...], NT, preferred_element_type=F32)
    first = jnp.where(lane == 255, mine, first)
    later = lax.dot_general(merged, cot[...], NT, preferred_element_type=F32)
    kept = jnp.where(core == 0, first, later)
    sent = jnp.where(core == 0, later, first)
    for half in range(2):
        keep[32 * half : 32 * half + 32, :] = kept[:, half * TILE : (half + 1) * TILE]
        send[32 * half : 32 * half + 32, :] = sent[:, half * TILE : (half + 1) * TILE]


def score(place, cols, hidden, dhidden, tiles, cot, self_t, neigh_t):
    shape = jax.ShapeDtypeStruct((64, TILE), F32)
    return pl.pallas_call(
        score_kernel,
        in_specs=[SMEM, SMEM] + [VMEM] * 6,
        out_specs=[VMEM] * 3,
        scratch_shapes=[pltpu.VMEM((tiles.shape[0], TILE, TILE), BF)],
        out_shape=[jax.ShapeDtypeStruct((8, 48, TILE), BF), shape, shape],
        compiler_params=LIMIT,
    )(place, cols, hidden, dhidden, tiles, cot, self_t, neigh_t)


def fan_kernel(parts, out):
    total = parts[0].astype(F32)
    for j in range(1, parts.shape[0]):
        total = total + parts[j].astype(F32)
    for d in range(out.shape[0]):
        out[d] = total.astype(BF)


def fan(parts):
    return pl.pallas_call(
        fan_kernel,
        in_specs=[VMEM],
        out_specs=VMEM,
        out_shape=jax.ShapeDtypeStruct((32,) + parts.shape[1:], BF),
        compiler_params=LIMIT,
    )(parts)


def logit_kernel(parts, out):
    classes = out.shape[0]
    for j in range(8):
        rows = min(24, classes - 24 * j)
        if rows <= 0:
            continue
        for zq in range(4):
            block = parts[8 * zq + j].astype(F32)
            for half in range(2):
                at = (2 * zq + half) * TILE
                out[24 * j : 24 * j + rows, at : at + TILE] = block[24 * half : 24 * half + rows]


def join(parts, classes, slots):
    return pl.pallas_call(
        logit_kernel,
        in_specs=[VMEM],
        out_specs=VMEM,
        out_shape=jax.ShapeDtypeStruct((classes, slots), F32),
        compiler_params=LIMIT,
    )(parts)


def grad_kernel(place, hidden, dhidden, f0, f1, f2, f3, g0, g1, g2, g3, keep, send, total):
    core, zr, y = place[0], place[3], place[4]
    blocks, deep, _ = f0.shape
    half = deep // 2
    parts = (f0, f1, f2, f3, g0, g1, g2, g3)
    total[...] = jnp.zeros_like(total)

    def grow(b, carry):
        low = jnp.where(hidden[b].astype(F32) > 0.0, dhidden[b], 0.0).astype(BF)
        stack = jnp.concatenate([part[b] for part in parts], axis=0)
        total[...] += lax.dot_general(stack, low, NT, preferred_element_type=F32)
        return carry

    lax.fori_loop(0, blocks, grow, 0, unroll=4)
    for j in range(len(parts)):
        owner = 4 * (zr if j < 4 else 1 - zr) + lax.rem(y + 8 - j, 4)
        keep[owner] = total[pl.ds(pl.multiple_of(j * deep + core * half, 8), half), :]
        send[owner] = total[pl.ds(pl.multiple_of(j * deep + (1 - core) * half, 8), half), :]


def grad(place, hidden, dhidden, feats):
    _, deep, _ = feats[0].shape
    shape = jax.ShapeDtypeStruct((8, deep // 2, TILE), F32)
    return pl.pallas_call(
        grad_kernel,
        in_specs=[SMEM] + [VMEM] * 10,
        out_specs=[VMEM, VMEM],
        scratch_shapes=[pltpu.VMEM((8 * deep, TILE), F32)],
        out_shape=[shape, shape],
        compiler_params=LIMIT,
        cost_estimate=pl.CostEstimate(flops=10**9, bytes_accessed=7 * 10**6, transcendentals=0),
    )(place, hidden, dhidden, *feats)


def finish_kernel(place, keep, rest, grad_self, grad_neigh, head_self, head_neigh, bias):
    core = place[0]
    deep = grad_self.shape[0]
    classes = head_self.shape[1]
    first = jnp.where(core == 0, keep[...], rest[...])
    later = jnp.where(core == 0, rest[...], keep[...])
    for value, weight, head in ((first, grad_self, head_self), (later, grad_neigh, head_neigh)):
        for zq in range(4):
            for zr in range(2):
                pieces = [
                    value[(4 * zr + y) * deep : (4 * zr + y + 1) * deep, 32 * zq : 32 * zq + 32]
                    for y in range(4)
                ]
                at = (2 * zq + zr) * TILE
                weight[:, at : at + TILE] = jnp.concatenate(pieces, axis=1)
        base = 8 * deep
        head[:, 0:TILE] = value[base : base + 32]
        head[:, TILE:classes] = value[base + 32 : base + 64, 0 : classes - TILE]
    bias[...] = first[8 * deep + 32 : 8 * deep + 64, TILE - 1 : TILE]


def finish(place, keep, rest, deep, classes):
    weight = jax.ShapeDtypeStruct((deep, 1024), F32)
    head = jax.ShapeDtypeStruct((32, classes), F32)
    return pl.pallas_call(
        finish_kernel,
        in_specs=[SMEM, VMEM, VMEM],
        out_specs=[VMEM] * 5,
        out_shape=[weight, weight, head, head, jax.ShapeDtypeStruct((32, 1), F32)],
        compiler_params=LIMIT,
    )(place, keep, rest)


def shift(value, axis, by):
    return lax.ppermute(value, axis, [(i, (i + by) % 4) for i in range(4)])


def swap(value, axis):
    return lax.ppermute(value, axis, [(0, 1), (1, 0)])


def sum_x(value):
    value = value + lax.ppermute(value, "x", [(0, 1), (1, 0), (2, 3), (3, 2)])
    return value + lax.ppermute(value, "x", [(0, 3), (3, 0), (1, 2), (2, 1)])


def shards(
    feature_table,
    node_ids,
    hop_cols,
    hop_tiles,
    target_cols,
    target_tiles,
    self_weight,
    neigh_weight,
    hidden_bias,
    head_self,
    head_neigh,
    batch_sizes,
    logit_cotangent,
):
    blocks = hop_cols.shape[0]
    deep = feature_table.shape[0]
    classes, target_rows = logit_cotangent.shape
    place = jnp.stack([lax.axis_index(axis) for axis in ("core", "x") + FEAT])

    packed, pair = pack(place, self_weight, neigh_weight, head_self, head_neigh)
    weights = lax.all_to_all(packed, FEAT, 0, 0, tiled=True)
    send, feats = hop(
        place, feature_table, node_ids, hop_cols, hidden_bias, hop_tiles, packed
    )
    weights, pair, send, feats = lax.optimization_barrier((weights, pair, send, feats))
    got = lax.all_to_all(send, FEAT, 0, 0, tiled=True)
    weights = weights.reshape(-1, 512)
    mine = [weights, shift(weights[:, :256], "x", 1), shift(weights[:, 256:], "x", 3)]
    other = [swap(w, "core") for w in mine]

    twin = swap(feats, "zr")
    feats = [feats] + [shift(feats, "y", s) for s in (1, 2, 3)]

    hidden = layer(place, got, mine, other)
    hidden, pair, twin, feats = lax.optimization_barrier((hidden, pair, twin, feats))
    hidden = lax.all_to_all(hidden, FEAT, 0, 0, tiled=True)
    pairs = [pair] + [shift(pair, "zq", s) for s in (1, 2, 3)]
    feats = feats + [twin] + [shift(twin, "y", s) for s in (1, 2, 3)]
    live = batch_sizes[lax.axis_index("x") * 2 + lax.axis_index("core")]
    dhidden, cot, self_t, neigh_t = spread(
        place, target_cols, live, logit_cotangent, pairs, target_tiles, blocks
    )

    scores, keep_head, send_head = score(
        place, target_cols, hidden, dhidden, target_tiles, cot, self_t, neigh_t
    )
    scores = lax.all_to_all(scores, ("zr", "y"), 0, 0, tiled=True)
    keep_head = keep_head + swap(send_head, "core")
    keep, send = grad(place, hidden, dhidden, feats)
    keep = keep + swap(send, "core")
    keep = lax.all_to_all(keep, ("zr", "y"), 0, 0, tiled=True)
    scores = lax.all_to_all(fan(scores), FEAT, 0, 0, tiled=True)
    keep = sum_x(jnp.concatenate([keep.reshape(-1, TILE), keep_head], axis=0))
    results = finish(place, keep, swap(keep, "core"), deep, classes)
    return (join(scores, classes, target_rows), *results[:4], results[4].reshape(-1))


def solution(mesh):
    split = Mesh(mesh.devices.reshape(4, 2, 4, 2, 4), DP + FEAT)
    return jax.shard_map(
        shards,
        mesh=split,
        in_specs=(
            P(FEAT, None),
            P(DP),
            P(DP, None),
            P(DP, None, None, None),
            P(DP, None),
            P(DP, None, None, None),
            P(FEAT, None),
            P(FEAT, None),
            P(FEAT),
            P(FEAT, None),
            P(FEAT, None),
            P(),
            P(None, DP),
        ),
        out_specs=(
            P(None, DP),
            P(FEAT, None),
            P(FEAT, None),
            P(FEAT, None),
            P(FEAT, None),
            P(FEAT),
        ),
        check_vma=False,
    )
```

```python
import jax
import jax.numpy as jnp
from jax import lax
from jax.experimental import pallas as pl
from jax.experimental.pallas import tpu as pltpu
from jax.sharding import Mesh, PartitionSpec as P

TILE = 128
FEAT = ("zq", "zr", "y")
DP = ("x", "core")
BF = jnp.bfloat16
F32 = jnp.float32
NT = (((1,), (1,)), ((), ()))
VMEM = pl.BlockSpec(memory_space=pltpu.VMEM)
SMEM = pl.BlockSpec(memory_space=pltpu.SMEM)
HBM = pl.BlockSpec(memory_space=pl.ANY)
LIMIT = pltpu.CompilerParams(vmem_limit_bytes=56 * 2**20)


def aligned(index, size):
    return pl.ds(pl.multiple_of(index * size, size), size)


def split_bias(bias):
    row = lax.broadcasted_iota(jnp.int32, (8, bias.shape[1]), 0)
    left = jnp.broadcast_to(bias, row.shape)
    high = left.astype(BF).astype(F32)
    left = left - high
    middle = left.astype(BF).astype(F32)
    low = left - middle
    return jnp.where(row == 0, high, jnp.where(row == 1, middle, jnp.where(row == 2, low, 0.0)))


def hop_kernel(place, ids, cols, table, bias, tiles_hbm, _, out, feats, rows, picked, tiles, sem):
    width = table.shape[0]
    blocks = tiles.shape[0]
    group = blocks // 8
    copies = [
        pltpu.make_async_copy(
            tiles_hbm.at[pl.ds(j * group, group)], tiles.at[pl.ds(j * group, group)], sem.at[j]
        )
        for j in range(8)
    ]
    for copy in copies:
        copy.start()

    def turn(b, carry):
        rows[aligned(b, TILE), 0:width] = table[:, aligned(b, TILE)].astype(F32).T
        return carry

    lax.fori_loop(0, table.shape[1] // TILE, turn, 0, unroll=8)
    step = 64

    def pick(g, carry):
        base = pl.multiple_of(g * step, step)
        for u in range(step):
            picked[pl.ds(base + u, 1), :] = rows[pl.ds(ids[base + u], 1), :]
        return carry

    lax.fori_loop(0, ids.shape[0] // step, pick, 0)
    lane = lax.broadcasted_iota(jnp.int32, (8, TILE), 1)
    term = split_bias(jnp.concatenate([bias[...]] * 4, axis=1))
    term = jnp.where(lane // 32 == place[4], term, 0.0)
    for copy in copies:
        copy.wait()

    def merge(r, carry):
        own = picked[aligned(r, TILE), :].T[0:width]
        left = jnp.concatenate([tiles[r, k] for k in range(8)], axis=1)
        right = jnp.concatenate(
            [picked[aligned(cols[r, k], TILE), :].astype(BF) for k in range(8)], axis=0
        )
        total = jnp.dot(left, right, preferred_element_type=F32)
        both = jnp.concatenate([own, total.T[0:width]], axis=0)
        feats[r] = both.astype(BF)
        out[r] = jnp.concatenate([both, term], axis=0).astype(BF)
        return carry

    lax.fori_loop(0, blocks, merge, 0, unroll=2)


def hop(place, table, ids, cols, bias, tiles, after):
    blocks, deep = tiles.shape[0], 2 * table.shape[0]
    return pl.pallas_call(
        hop_kernel,
        in_specs=[SMEM, SMEM, SMEM, VMEM, VMEM, HBM, HBM],
        out_specs=[VMEM, VMEM],
        scratch_shapes=[
            pltpu.VMEM((table.shape[1], TILE), F32),
            pltpu.VMEM((ids.shape[0], TILE), F32),
            pltpu.VMEM(tiles.shape, BF),
            pltpu.SemaphoreType.DMA((8,)),
        ],
        out_shape=[
            jax.ShapeDtypeStruct((blocks, deep + 8, TILE), BF),
            jax.ShapeDtypeStruct((blocks, deep, TILE), BF),
        ],
        compiler_params=LIMIT,
        cost_estimate=pl.CostEstimate(flops=10**9, bytes_accessed=60 * 10**6, transcendentals=0),
    )(place, ids, cols, table, bias.reshape(1, -1), tiles, after)


def pack_kernel(place, own, neigh, head_self, head_neigh, weights, heads):
    core, x = place[0], place[1]
    cols = aligned(lax.rem(x, 2), 512)
    block = jnp.where(core == 0, own[:, cols].astype(F32), neigh[:, cols].astype(F32)).astype(BF)
    for d in range(weights.shape[0]):
        weights[d] = block
    classes = head_self.shape[1]
    heads[...] = jnp.zeros_like(heads)
    heads[0:32, 0:classes] = head_self[...]
    heads[32:64, 0:classes] = head_neigh[...]


def pack(place, own, neigh, head_self, head_neigh):
    return pl.pallas_call(
        pack_kernel,
        in_specs=[SMEM] + [VMEM] * 4,
        out_specs=[VMEM, VMEM],
        out_shape=[
            jax.ShapeDtypeStruct((32, own.shape[0], 512), BF),
            jax.ShapeDtypeStruct((64, 256), BF),
        ],
        compiler_params=LIMIT,
    )(place, own, neigh, head_self, head_neigh)


def spread_kernel(
    place, cols, live, logit_cot, p0, p1, p2, p3, tiles, out, cot, self_t, neigh_t, own, neigh
):
    classes, slots = logit_cot.shape
    lane = lax.broadcasted_iota(jnp.int32, (classes, slots), 1)
    kept = jnp.where(lane < live[0], logit_cot[...].astype(F32), 0.0)
    cot[...] = jnp.concatenate([kept, jnp.zeros((256 - classes, slots), F32)], axis=0).astype(BF)
    out[...] = jnp.zeros_like(out)
    for s, part in enumerate((p0, p1, p2, p3)):
        at = aligned(lax.rem(place[2] + 4 - s, 4), 32)
        own[at, :] = part[0:32]
        neigh[at, :] = part[32:64]
    self_t[...] = own[...].astype(F32).T.astype(BF)
    neigh_t[...] = neigh[...].astype(F32).T.astype(BF)
    for r in range(tiles.shape[0]):
        part = cot[:, r * TILE : (r + 1) * TILE]
        out[r] = jnp.dot(own[...], part, preferred_element_type=F32)
    for r in range(tiles.shape[0]):
        part = cot[:, r * TILE : (r + 1) * TILE]
        back = jnp.dot(neigh[...], part, preferred_element_type=F32).astype(BF)
        for k in range(8):
            out[cols[r, k]] += jnp.dot(back, tiles[r, k], preferred_element_type=F32)


def spread(place, cols, live, logit_cot, pairs, tiles, blocks):
    return pl.pallas_call(
        spread_kernel,
        in_specs=[SMEM, SMEM, SMEM] + [VMEM] * 6,
        out_specs=[VMEM] * 4,
        scratch_shapes=[pltpu.VMEM((TILE, 256), BF)] * 2,
        out_shape=[
            jax.ShapeDtypeStruct((blocks, TILE, TILE), F32),
            jax.ShapeDtypeStruct((256, logit_cot.shape[1]), BF),
            jax.ShapeDtypeStruct((256, TILE), BF),
            jax.ShapeDtypeStruct((256, TILE), BF),
        ],
        compiler_params=LIMIT,
        cost_estimate=pl.CostEstimate(flops=10**9, bytes_accessed=8 * 10**6, transcendentals=0),
    )(place, cols, live.reshape(1), logit_cot, *pairs, tiles)


def layer_kernel(place, got, w0, w1, w2, o0, o1, o2, out, mine, other):
    core, x = place[0], place[1]
    deep = w0.shape[0] // 32
    for j in range(8):
        pieces = [got[4 * j + i].astype(F32) for i in range(4)]
        own = jnp.concatenate([piece[0:deep] for piece in pieces], axis=0).T.astype(BF)
        agg = jnp.concatenate([piece[deep : 2 * deep] for piece in pieces], axis=0).T.astype(BF)
        at = slice(j * 4 * deep, (j + 1) * 4 * deep)
        mine[:, at] = jnp.where(core == 0, own, agg)
        other[:, at] = jnp.where(core == 0, agg, own)

    def emit(chunk, w, o):
        preact = jnp.dot(mine[...], w, preferred_element_type=F32)
        preact = preact + jnp.dot(other[...], o, preferred_element_type=F32)
        rows = aligned(chunk, 32)
        for half in range(2):
            z = 2 * chunk + half
            terms = sum(got[4 * z + i].astype(F32)[2 * deep :] for i in range(4))
            bias = jnp.sum(terms, axis=0, keepdims=True)
            hidden = jnp.maximum(preact[:, half * TILE : (half + 1) * TILE] + bias, 0.0)
            hidden = hidden.T.astype(BF)
            for y in range(4):
                for zq in range(4):
                    out[8 * zq + 4 * half + y, rows, :] = hidden[32 * y : 32 * y + 32]

    near = 2 * lax.rem(x, 2)
    far = 2 - near
    emit(near, w0[:, 0:256], o0[:, 0:256])
    emit(near + 1, w0[:, 256:512], o0[:, 256:512])
    emit(far, w1[...], o1[...])
    emit(far + 1, w2[...], o2[...])


def layer(place, got, mine, other):
    return pl.pallas_call(
        layer_kernel,
        in_specs=[SMEM] + [VMEM] * 7,
        out_specs=VMEM,
        scratch_shapes=[pltpu.VMEM((TILE, mine[0].shape[0]), BF)] * 2,
        out_shape=jax.ShapeDtypeStruct((32, TILE, TILE), BF),
        compiler_params=LIMIT,
    )(place, got, *mine, *other)


def score_kernel(
    place, cols, hidden, dhidden, tiles, cot, self_t, neigh_t, out, keep, send, second
):
    core, zq = place[0], place[2]
    own = aligned(zq, 32)
    for r in range(tiles.shape[0]):
        left = jnp.concatenate([hidden[cols[r, k]] for k in range(8)], axis=1)
        right = jnp.concatenate([tiles[r, k] for k in range(8)], axis=1)
        second[r] = lax.dot_general(left, right, NT, preferred_element_type=F32).astype(BF)
    halves = []
    for half in range(2):
        at = 2 * zq + half
        scores = jnp.dot(self_t[...], hidden[at], preferred_element_type=F32)
        halves.append(scores + jnp.dot(neigh_t[...], second[at], preferred_element_type=F32))
    block = jnp.concatenate(halves, axis=1)[0 : out.shape[1]].astype(BF)
    for z in range(out.shape[0]):
        out[z] = block
    total = jnp.zeros((32, TILE), F32)
    for b in range(hidden.shape[0]):
        total = total + jnp.where(hidden[b, own, :].astype(F32) > 0.0, dhidden[b, own, :], 0.0)
    mine = jnp.sum(total, axis=1, keepdims=True)
    targets = jnp.concatenate([hidden[r, own, :] for r in range(tiles.shape[0])], axis=1)
    merged = jnp.concatenate([second[r, own, :] for r in range(tiles.shape[0])], axis=1)
    lane = lax.broadcasted_iota(jnp.int32, (32, 256), 1)
    first = lax.dot_general(targets, cot[...], NT, preferred_element_type=F32)
    first = jnp.where(lane == 255, mine, first)
    later = lax.dot_general(merged, cot[...], NT, preferred_element_type=F32)
    kept = jnp.where(core == 0, first, later)
    sent = jnp.where(core == 0, later, first)
    for half in range(2):
        keep[32 * half : 32 * half + 32, :] = kept[:, half * TILE : (half + 1) * TILE]
        send[32 * half : 32 * half + 32, :] = sent[:, half * TILE : (half + 1) * TILE]


def score(place, cols, hidden, dhidden, tiles, cot, self_t, neigh_t):
    shape = jax.ShapeDtypeStruct((64, TILE), F32)
    return pl.pallas_call(
        score_kernel,
        in_specs=[SMEM, SMEM] + [VMEM] * 6,
        out_specs=[VMEM] * 3,
        scratch_shapes=[pltpu.VMEM((tiles.shape[0], TILE, TILE), BF)],
        out_shape=[jax.ShapeDtypeStruct((8, 160, 256), BF), shape, shape],
        compiler_params=LIMIT,
    )(place, cols, hidden, dhidden, tiles, cot, self_t, neigh_t)


def total_kernel(parts, out):
    total = parts[0].astype(F32)
    for j in range(1, parts.shape[0]):
        total = total + parts[j].astype(F32)
    out[...] = total.astype(BF)


def total(parts):
    return pl.pallas_call(
        total_kernel,
        in_specs=[VMEM],
        out_specs=VMEM,
        out_shape=jax.ShapeDtypeStruct(parts.shape[1:], BF),
        compiler_params=LIMIT,
    )(parts)


def logit_kernel(place, s0, s1, s2, s3, out):
    classes = out.shape[0]
    for s, part in enumerate((s0, s1, s2, s3)):
        at = aligned(lax.rem(place[2] + 4 - s, 4), 256)
        out[:, at] = part[...].astype(F32)[0:classes]


def join(place, parts, classes):
    return pl.pallas_call(
        logit_kernel,
        in_specs=[SMEM] + [VMEM] * 4,
        out_specs=VMEM,
        out_shape=jax.ShapeDtypeStruct((classes, 4 * parts[0].shape[1]), F32),
        compiler_params=LIMIT,
    )(place, *parts)


def grad_kernel(place, hidden, dhidden, f0, f1, f2, f3, g0, g1, g2, g3, keep, send, total):
    core, zr, y = place[0], place[3], place[4]
    blocks, deep, _ = f0.shape
    half = deep // 2
    parts = (f0, f1, f2, f3, g0, g1, g2, g3)
    total[...] = jnp.zeros_like(total)

    def grow(b, carry):
        low = jnp.where(hidden[b].astype(F32) > 0.0, dhidden[b], 0.0).astype(BF)
        stack = jnp.concatenate([part[b] for part in parts], axis=0)
        total[...] += lax.dot_general(stack, low, NT, preferred_element_type=F32)
        return carry

    lax.fori_loop(0, blocks, grow, 0, unroll=4)
    for j in range(len(parts)):
        owner = 4 * (zr if j < 4 else 1 - zr) + lax.rem(y + 8 - j, 4)
        keep[owner] = total[pl.ds(pl.multiple_of(j * deep + core * half, 8), half), :]
        send[owner] = total[pl.ds(pl.multiple_of(j * deep + (1 - core) * half, 8), half), :]


def grad(place, hidden, dhidden, feats):
    _, deep, _ = feats[0].shape
    shape = jax.ShapeDtypeStruct((8, deep // 2, TILE), F32)
    return pl.pallas_call(
        grad_kernel,
        in_specs=[SMEM] + [VMEM] * 10,
        out_specs=[VMEM, VMEM],
        scratch_shapes=[pltpu.VMEM((8 * deep, TILE), F32)],
        out_shape=[shape, shape],
        compiler_params=LIMIT,
        cost_estimate=pl.CostEstimate(flops=10**9, bytes_accessed=7 * 10**6, transcendentals=0),
    )(place, hidden, dhidden, *feats)


def finish_kernel(place, keep, rest, grad_self, grad_neigh, head_self, head_neigh, bias):
    core = place[0]
    deep = grad_self.shape[0]
    classes = head_self.shape[1]
    first = jnp.where(core == 0, keep[...], rest[...])
    later = jnp.where(core == 0, rest[...], keep[...])
    for value, weight, head in ((first, grad_self, head_self), (later, grad_neigh, head_neigh)):
        for zq in range(4):
            for zr in range(2):
                pieces = [
                    value[(4 * zr + y) * deep : (4 * zr + y + 1) * deep, 32 * zq : 32 * zq + 32]
                    for y in range(4)
                ]
                at = (2 * zq + zr) * TILE
                weight[:, at : at + TILE] = jnp.concatenate(pieces, axis=1)
        base = 8 * deep
        head[:, 0:TILE] = value[base : base + 32]
        head[:, TILE:classes] = value[base + 32 : base + 64, 0 : classes - TILE]
    bias[...] = first[8 * deep + 32 : 8 * deep + 64].T[TILE - 1 : TILE]


def finish(place, keep, rest, deep, classes):
    weight = jax.ShapeDtypeStruct((deep, 1024), F32)
    head = jax.ShapeDtypeStruct((32, classes), F32)
    return pl.pallas_call(
        finish_kernel,
        in_specs=[SMEM, VMEM, VMEM],
        out_specs=[VMEM] * 5,
        out_shape=[weight, weight, head, head, jax.ShapeDtypeStruct((1, 32), F32)],
        compiler_params=LIMIT,
    )(place, keep, rest)


def shift(value, axis, by):
    return lax.ppermute(value, axis, [(i, (i + by) % 4) for i in range(4)])


def swap(value, axis):
    return lax.ppermute(value, axis, [(0, 1), (1, 0)])


def sum_x(value):
    value = value + lax.ppermute(value, "x", [(0, 1), (1, 0), (2, 3), (3, 2)])
    return value + lax.ppermute(value, "x", [(0, 3), (3, 0), (1, 2), (2, 1)])


def shards(
    feature_table,
    node_ids,
    hop_cols,
    hop_tiles,
    target_cols,
    target_tiles,
    self_weight,
    neigh_weight,
    hidden_bias,
    head_self,
    head_neigh,
    batch_sizes,
    logit_cotangent,
):
    blocks = hop_cols.shape[0]
    deep = feature_table.shape[0]
    classes, target_rows = logit_cotangent.shape
    place = jnp.stack([lax.axis_index(axis) for axis in ("core", "x") + FEAT])

    packed, pair = pack(place, self_weight, neigh_weight, head_self, head_neigh)
    weights = lax.all_to_all(packed, FEAT, 0, 0, tiled=True)
    send, feats = hop(
        place, feature_table, node_ids, hop_cols, hidden_bias, hop_tiles, packed
    )
    pairs = [pair] + [shift(pair, "zq", s) for s in (1, 2, 3)]
    weights, pairs, send, feats = lax.optimization_barrier((weights, pairs, send, feats))
    got = lax.all_to_all(send, FEAT, 0, 0, tiled=True)
    weights = weights.reshape(-1, 512)
    mine = [weights, shift(weights[:, :256], "x", 1), shift(weights[:, 256:], "x", 3)]
    other = [swap(w, "core") for w in mine]

    twin = swap(feats, "zr")

    live = batch_sizes[lax.axis_index("x") * 2 + lax.axis_index("core")]
    ready = spread(place, target_cols, live, logit_cotangent, pairs, target_tiles, blocks)
    hidden = layer(place, got, mine, other)
    hidden, ready, feats, twin = lax.optimization_barrier((hidden, ready, feats, twin))
    dhidden, cot, self_t, neigh_t = ready
    hidden = lax.all_to_all(hidden, FEAT, 0, 0, tiled=True)
    feats = [feats] + [shift(feats, "y", s) for s in (1, 2, 3)]
    feats = feats + [twin] + [shift(twin, "y", s) for s in (1, 2, 3)]
    hidden, feats = lax.optimization_barrier((hidden, feats))

    scores, keep_head, send_head = score(
        place, target_cols, hidden, dhidden, target_tiles, cot, self_t, neigh_t
    )
    scores = lax.all_to_all(scores, ("zr", "y"), 0, 0, tiled=True)
    hidden, keep_head, send_head = lax.optimization_barrier((hidden, keep_head, send_head))
    keep_head = keep_head + swap(send_head, "core")
    keep, send = grad(place, hidden, dhidden, feats)
    keep = keep + swap(send, "core")
    keep, scores, keep_head = lax.optimization_barrier((keep, scores, keep_head))
    keep = lax.all_to_all(keep, ("zr", "y"), 0, 0, tiled=True)
    scores = total(scores)
    scores = [scores] + [shift(scores, "zq", s) for s in (1, 2, 3)]
    keep, scores = lax.optimization_barrier((keep, scores))
    keep = sum_x(jnp.concatenate([keep.reshape(-1, TILE), keep_head], axis=0))
    results = finish(place, keep, swap(keep, "core"), deep, classes)
    return (join(place, scores, classes), *results[:4], results[4].reshape(-1))


def solution(mesh):
    split = Mesh(mesh.devices.reshape(4, 2, 4, 2, 4), DP + FEAT)
    return jax.shard_map(
        shards,
        mesh=split,
        in_specs=(
            P(FEAT, None),
            P(DP),
            P(DP, None),
            P(DP, None, None, None),
            P(DP, None),
            P(DP, None, None, None),
            P(FEAT, None),
            P(FEAT, None),
            P(FEAT),
            P(FEAT, None),
            P(FEAT, None),
            P(),
            P(None, DP),
        ),
        out_specs=(
            P(None, DP),
            P(FEAT, None),
            P(FEAT, None),
            P(FEAT, None),
            P(FEAT, None),
            P(FEAT),
        ),
        check_vma=False,
    )
```

```python
import jax
import jax.numpy as jnp
from jax import lax
from jax.experimental import pallas as pl
from jax.experimental.pallas import tpu as pltpu
from jax.sharding import Mesh, PartitionSpec as P

TILE = 128
FEAT = ("zq", "zr", "y")
DP = ("x", "core")
BF = jnp.bfloat16
F32 = jnp.float32
NT = (((1,), (1,)), ((), ()))
VMEM = pl.BlockSpec(memory_space=pltpu.VMEM)
SMEM = pl.BlockSpec(memory_space=pltpu.SMEM)
HBM = pl.BlockSpec(memory_space=pl.ANY)
LIMIT = pltpu.CompilerParams(vmem_limit_bytes=56 * 2**20)


def aligned(index, size):
    return pl.ds(pl.multiple_of(index * size, size), size)


def split_bias(bias):
    row = lax.broadcasted_iota(jnp.int32, (8, bias.shape[1]), 0)
    left = jnp.broadcast_to(bias, row.shape)
    high = left.astype(BF).astype(F32)
    left = left - high
    middle = left.astype(BF).astype(F32)
    low = left - middle
    return jnp.where(row == 0, high, jnp.where(row == 1, middle, jnp.where(row == 2, low, 0.0)))


def hop_kernel(place, ids, cols, table, bias, tiles_hbm, _, out, feats, rows, picked, tiles, sem):
    width = table.shape[0]
    blocks = tiles.shape[0]
    group = blocks // 8
    copies = [
        pltpu.make_async_copy(
            tiles_hbm.at[pl.ds(j * group, group)], tiles.at[pl.ds(j * group, group)], sem.at[j]
        )
        for j in range(8)
    ]
    for copy in copies:
        copy.start()

    def turn(b, carry):
        rows[aligned(b, TILE), 0:width] = table[:, aligned(b, TILE)].astype(F32).T
        return carry

    lax.fori_loop(0, table.shape[1] // TILE, turn, 0, unroll=8)
    step = 64

    def pick(g, carry):
        base = pl.multiple_of(g * step, step)
        for u in range(step):
            picked[pl.ds(base + u, 1), :] = rows[pl.ds(ids[base + u], 1), :]
        return carry

    lax.fori_loop(0, ids.shape[0] // step, pick, 0)
    lane = lax.broadcasted_iota(jnp.int32, (8, TILE), 1)
    term = split_bias(jnp.concatenate([bias[...]] * 4, axis=1))
    term = jnp.where(lane // 32 == place[4], term, 0.0)
    for copy in copies:
        copy.wait()

    def merge(r, carry):
        own = picked[aligned(r, TILE), :].T[0:width]
        left = jnp.concatenate([tiles[r, k] for k in range(8)], axis=1)
        right = jnp.concatenate(
            [picked[aligned(cols[r, k], TILE), :].astype(BF) for k in range(8)], axis=0
        )
        total = jnp.dot(left, right, preferred_element_type=F32)
        both = jnp.concatenate([own, total.T[0:width]], axis=0)
        feats[r] = both.astype(BF)
        out[r] = jnp.concatenate([both, term], axis=0).astype(BF)
        return carry

    lax.fori_loop(0, blocks, merge, 0, unroll=2)


def hop(place, table, ids, cols, bias, tiles, after):
    blocks, deep = tiles.shape[0], 2 * table.shape[0]
    return pl.pallas_call(
        hop_kernel,
        in_specs=[SMEM, SMEM, SMEM, VMEM, VMEM, HBM, HBM],
        out_specs=[VMEM, VMEM],
        scratch_shapes=[
            pltpu.VMEM((table.shape[1], TILE), F32),
            pltpu.VMEM((ids.shape[0], TILE), F32),
            pltpu.VMEM(tiles.shape, BF),
            pltpu.SemaphoreType.DMA((8,)),
        ],
        out_shape=[
            jax.ShapeDtypeStruct((blocks, deep + 8, TILE), BF),
            jax.ShapeDtypeStruct((blocks, deep, TILE), BF),
        ],
        compiler_params=LIMIT,
        cost_estimate=pl.CostEstimate(flops=10**9, bytes_accessed=60 * 10**6, transcendentals=0),
    )(place, ids, cols, table, bias.reshape(1, -1), tiles, after)


def pack_kernel(place, own, neigh, head_self, head_neigh, weights, heads):
    core, x = place[0], place[1]
    cols = aligned(lax.rem(x, 2), 512)
    block = jnp.where(core == 0, own[:, cols].astype(F32), neigh[:, cols].astype(F32)).astype(BF)
    for d in range(weights.shape[0]):
        weights[d] = block
    classes = head_self.shape[1]
    heads[...] = jnp.zeros_like(heads)
    heads[0:32, 0:classes] = head_self[...]
    heads[32:64, 0:classes] = head_neigh[...]


def pack(place, own, neigh, head_self, head_neigh):
    return pl.pallas_call(
        pack_kernel,
        in_specs=[SMEM] + [VMEM] * 4,
        out_specs=[VMEM, VMEM],
        out_shape=[
            jax.ShapeDtypeStruct((32, own.shape[0], 512), BF),
            jax.ShapeDtypeStruct((64, 256), BF),
        ],
        compiler_params=LIMIT,
    )(place, own, neigh, head_self, head_neigh)


def spread_kernel(
    place, cols, live, logit_cot, p0, p1, p2, p3, tiles, out, cot, self_t, neigh_t, own, neigh
):
    classes, slots = logit_cot.shape
    lane = lax.broadcasted_iota(jnp.int32, (classes, slots), 1)
    kept = jnp.where(lane < live[0], logit_cot[...].astype(F32), 0.0)
    cot[...] = jnp.concatenate([kept, jnp.zeros((256 - classes, slots), F32)], axis=0).astype(BF)
    out[...] = jnp.zeros_like(out)
    for s, part in enumerate((p0, p1, p2, p3)):
        at = aligned(lax.rem(place[2] + 4 - s, 4), 32)
        own[at, :] = part[0:32]
        neigh[at, :] = part[32:64]
    self_t[...] = own[...].astype(F32).T.astype(BF)
    neigh_t[...] = neigh[...].astype(F32).T.astype(BF)
    for r in range(tiles.shape[0]):
        part = cot[:, r * TILE : (r + 1) * TILE]
        out[r] = jnp.dot(own[...], part, preferred_element_type=F32)
    for r in range(tiles.shape[0]):
        part = cot[:, r * TILE : (r + 1) * TILE]
        back = jnp.dot(neigh[...], part, preferred_element_type=F32).astype(BF)
        for k in range(8):
            out[cols[r, k]] += jnp.dot(back, tiles[r, k], preferred_element_type=F32)


def spread(place, cols, live, logit_cot, pairs, tiles, blocks):
    return pl.pallas_call(
        spread_kernel,
        in_specs=[SMEM, SMEM, SMEM] + [VMEM] * 6,
        out_specs=[VMEM] * 4,
        scratch_shapes=[pltpu.VMEM((TILE, 256), BF)] * 2,
        out_shape=[
            jax.ShapeDtypeStruct((blocks, TILE, TILE), F32),
            jax.ShapeDtypeStruct((256, logit_cot.shape[1]), BF),
            jax.ShapeDtypeStruct((256, TILE), BF),
            jax.ShapeDtypeStruct((256, TILE), BF),
        ],
        compiler_params=LIMIT,
        cost_estimate=pl.CostEstimate(flops=10**9, bytes_accessed=8 * 10**6, transcendentals=0),
    )(place, cols, live.reshape(1), logit_cot, *pairs, tiles)


def layer_kernel(place, got, w0, w1, w2, o0, o1, o2, out, mine, other):
    core, x = place[0], place[1]
    deep = w0.shape[0] // 32
    for j in range(8):
        pieces = [got[4 * j + i].astype(F32) for i in range(4)]
        own = jnp.concatenate([piece[0:deep] for piece in pieces], axis=0).T.astype(BF)
        agg = jnp.concatenate([piece[deep : 2 * deep] for piece in pieces], axis=0).T.astype(BF)
        at = slice(j * 4 * deep, (j + 1) * 4 * deep)
        mine[:, at] = jnp.where(core == 0, own, agg)
        other[:, at] = jnp.where(core == 0, agg, own)

    def emit(chunk, w, o):
        preact = jnp.dot(mine[...], w, preferred_element_type=F32)
        preact = preact + jnp.dot(other[...], o, preferred_element_type=F32)
        rows = aligned(chunk, 32)
        for half in range(2):
            z = 2 * chunk + half
            terms = sum(got[4 * z + i].astype(F32)[2 * deep :] for i in range(4))
            bias = jnp.sum(terms, axis=0, keepdims=True)
            hidden = jnp.maximum(preact[:, half * TILE : (half + 1) * TILE] + bias, 0.0)
            hidden = hidden.T.astype(BF)
            for y in range(4):
                for zq in range(4):
                    out[8 * zq + 4 * half + y, rows, :] = hidden[32 * y : 32 * y + 32]

    near = 2 * lax.rem(x, 2)
    far = 2 - near
    emit(near, w0[:, 0:256], o0[:, 0:256])
    emit(near + 1, w0[:, 256:512], o0[:, 256:512])
    emit(far, w1[...], o1[...])
    emit(far + 1, w2[...], o2[...])


def layer(place, got, mine, other):
    return pl.pallas_call(
        layer_kernel,
        in_specs=[SMEM] + [VMEM] * 7,
        out_specs=VMEM,
        scratch_shapes=[pltpu.VMEM((TILE, mine[0].shape[0]), BF)] * 2,
        out_shape=jax.ShapeDtypeStruct((32, TILE, TILE), BF),
        compiler_params=LIMIT,
    )(place, got, *mine, *other)


def score_kernel(
    place, cols, hidden, dhidden, tiles, cot, self_t, neigh_t, out, keep, send, second
):
    core, zq = place[0], place[2]
    own = aligned(zq, 32)
    for r in range(tiles.shape[0]):
        left = jnp.concatenate([hidden[cols[r, k]] for k in range(8)], axis=1)
        right = jnp.concatenate([tiles[r, k] for k in range(8)], axis=1)
        second[r] = lax.dot_general(left, right, NT, preferred_element_type=F32).astype(BF)
    halves = []
    for half in range(2):
        at = 2 * zq + half
        scores = jnp.dot(self_t[...], hidden[at], preferred_element_type=F32)
        halves.append(scores + jnp.dot(neigh_t[...], second[at], preferred_element_type=F32))
    block = jnp.concatenate(halves, axis=1)[0 : out.shape[1]].astype(BF)
    for z in range(out.shape[0]):
        out[z] = block
    total = jnp.zeros((32, TILE), F32)
    for b in range(hidden.shape[0]):
        total = total + jnp.where(hidden[b, own, :].astype(F32) > 0.0, dhidden[b, own, :], 0.0)
    mine = jnp.sum(total, axis=1, keepdims=True)
    targets = jnp.concatenate([hidden[r, own, :] for r in range(tiles.shape[0])], axis=1)
    merged = jnp.concatenate([second[r, own, :] for r in range(tiles.shape[0])], axis=1)
    lane = lax.broadcasted_iota(jnp.int32, (32, 256), 1)
    first = lax.dot_general(targets, cot[...], NT, preferred_element_type=F32)
    first = jnp.where(lane == 255, mine, first)
    later = lax.dot_general(merged, cot[...], NT, preferred_element_type=F32)
    kept = jnp.where(core == 0, first, later)
    sent = jnp.where(core == 0, later, first)
    for half in range(2):
        keep[32 * half : 32 * half + 32, :] = kept[:, half * TILE : (half + 1) * TILE]
        send[32 * half : 32 * half + 32, :] = sent[:, half * TILE : (half + 1) * TILE]


def score(place, cols, hidden, dhidden, tiles, cot, self_t, neigh_t):
    shape = jax.ShapeDtypeStruct((64, TILE), F32)
    return pl.pallas_call(
        score_kernel,
        in_specs=[SMEM, SMEM] + [VMEM] * 6,
        out_specs=[VMEM] * 3,
        scratch_shapes=[pltpu.VMEM((tiles.shape[0], TILE, TILE), BF)],
        out_shape=[jax.ShapeDtypeStruct((8, 160, 256), BF), shape, shape],
        compiler_params=LIMIT,
    )(place, cols, hidden, dhidden, tiles, cot, self_t, neigh_t)


def total_kernel(parts, out):
    total = parts[0].astype(F32)
    for j in range(1, parts.shape[0]):
        total = total + parts[j].astype(F32)
    out[...] = total.astype(BF)


def total(parts):
    return pl.pallas_call(
        total_kernel,
        in_specs=[VMEM],
        out_specs=VMEM,
        out_shape=jax.ShapeDtypeStruct(parts.shape[1:], BF),
        compiler_params=LIMIT,
    )(parts)


def logit_kernel(place, s0, s1, s2, s3, out):
    classes = out.shape[0]
    for s, part in enumerate((s0, s1, s2, s3)):
        at = aligned(lax.rem(place[2] + 4 - s, 4), 256)
        out[:, at] = part[...].astype(F32)[0:classes]


def join(place, parts, classes):
    return pl.pallas_call(
        logit_kernel,
        in_specs=[SMEM] + [VMEM] * 4,
        out_specs=VMEM,
        out_shape=jax.ShapeDtypeStruct((classes, 4 * parts[0].shape[1]), F32),
        compiler_params=LIMIT,
    )(place, *parts)


def grad_kernel(place, hidden, dhidden, f0, f1, f2, f3, g0, g1, g2, g3, keep, send, total):
    core, zr, y = place[0], place[3], place[4]
    blocks, deep, _ = f0.shape
    half = deep // 2
    parts = (f0, f1, f2, f3, g0, g1, g2, g3)
    total[...] = jnp.zeros_like(total)

    def grow(b, carry):
        low = jnp.where(hidden[b].astype(F32) > 0.0, dhidden[b], 0.0).astype(BF)
        stack = jnp.concatenate([part[b] for part in parts], axis=0)
        total[...] += lax.dot_general(stack, low, NT, preferred_element_type=F32)
        return carry

    lax.fori_loop(0, blocks, grow, 0, unroll=4)
    for j in range(len(parts)):
        owner = 4 * (zr if j < 4 else 1 - zr) + lax.rem(y + 8 - j, 4)
        keep[owner] = total[pl.ds(pl.multiple_of(j * deep + core * half, 8), half), :]
        send[owner] = total[pl.ds(pl.multiple_of(j * deep + (1 - core) * half, 8), half), :]


def grad(place, hidden, dhidden, feats):
    _, deep, _ = feats[0].shape
    shape = jax.ShapeDtypeStruct((8, deep // 2, TILE), F32)
    return pl.pallas_call(
        grad_kernel,
        in_specs=[SMEM] + [VMEM] * 10,
        out_specs=[VMEM, VMEM],
        scratch_shapes=[pltpu.VMEM((8 * deep, TILE), F32)],
        out_shape=[shape, shape],
        compiler_params=LIMIT,
        cost_estimate=pl.CostEstimate(flops=10**9, bytes_accessed=7 * 10**6, transcendentals=0),
    )(place, hidden, dhidden, *feats)


def finish_kernel(place, keep, rest, grad_self, grad_neigh, head_self, head_neigh, bias):
    core = place[0]
    deep = grad_self.shape[0]
    classes = head_self.shape[1]
    first = jnp.where(core == 0, keep[...], rest[...])
    later = jnp.where(core == 0, rest[...], keep[...])
    for value, weight, head in ((first, grad_self, head_self), (later, grad_neigh, head_neigh)):
        for zq in range(4):
            for zr in range(2):
                pieces = [
                    value[(4 * zr + y) * deep : (4 * zr + y + 1) * deep, 32 * zq : 32 * zq + 32]
                    for y in range(4)
                ]
                at = (2 * zq + zr) * TILE
                weight[:, at : at + TILE] = jnp.concatenate(pieces, axis=1)
        base = 8 * deep
        head[:, 0:TILE] = value[base : base + 32]
        head[:, TILE:classes] = value[base + 32 : base + 64, 0 : classes - TILE]
    bias[...] = first[8 * deep + 32 : 8 * deep + 64].T[TILE - 1 : TILE]


def finish(place, keep, rest, deep, classes):
    weight = jax.ShapeDtypeStruct((deep, 1024), F32)
    head = jax.ShapeDtypeStruct((32, classes), F32)
    return pl.pallas_call(
        finish_kernel,
        in_specs=[SMEM, VMEM, VMEM],
        out_specs=[VMEM] * 5,
        out_shape=[weight, weight, head, head, jax.ShapeDtypeStruct((1, 32), F32)],
        compiler_params=LIMIT,
    )(place, keep, rest)


def shift(value, axis, by):
    return lax.ppermute(value, axis, [(i, (i + by) % 4) for i in range(4)])


def swap(value, axis):
    return lax.ppermute(value, axis, [(0, 1), (1, 0)])


def sum_x(value):
    value = value + lax.ppermute(value, "x", [(0, 1), (1, 0), (2, 3), (3, 2)])
    return value + lax.ppermute(value, "x", [(0, 3), (3, 0), (1, 2), (2, 1)])


def shards(
    feature_table,
    node_ids,
    hop_cols,
    hop_tiles,
    target_cols,
    target_tiles,
    self_weight,
    neigh_weight,
    hidden_bias,
    head_self,
    head_neigh,
    batch_sizes,
    logit_cotangent,
):
    blocks = hop_cols.shape[0]
    deep = feature_table.shape[0]
    classes, target_rows = logit_cotangent.shape
    place = jnp.stack([lax.axis_index(axis) for axis in ("core", "x") + FEAT])

    packed, pair = pack(place, self_weight, neigh_weight, head_self, head_neigh)
    weights = lax.all_to_all(packed, FEAT, 0, 0, tiled=True)
    send, feats = hop(
        place, feature_table, node_ids, hop_cols, hidden_bias, hop_tiles, packed
    )
    weights, pair, send, feats = lax.optimization_barrier((weights, pair, send, feats))
    got = lax.all_to_all(send, FEAT, 0, 0, tiled=True)
    weights = weights.reshape(-1, 512)
    mine = [weights, shift(weights[:, :256], "x", 1), shift(weights[:, 256:], "x", 3)]
    other = [swap(w, "core") for w in mine]

    twin = swap(feats, "zr")
    feats = [feats] + [shift(feats, "y", s) for s in (1, 2, 3)]
    got, feats, twin = lax.optimization_barrier((got, feats, twin))
    pairs = [pair] + [shift(pair, "zq", s) for s in (1, 2, 3)]

    hidden = layer(place, got, mine, other)
    hidden, pairs, twin = lax.optimization_barrier((hidden, pairs, twin))
    hidden = lax.all_to_all(hidden, FEAT, 0, 0, tiled=True)
    feats = feats + [twin] + [shift(twin, "y", s) for s in (1, 2, 3)]
    live = batch_sizes[lax.axis_index("x") * 2 + lax.axis_index("core")]
    dhidden, cot, self_t, neigh_t = spread(
        place, target_cols, live, logit_cotangent, pairs, target_tiles, blocks
    )
    hidden, feats = lax.optimization_barrier((hidden, feats))

    scores, keep_head, send_head = score(
        place, target_cols, hidden, dhidden, target_tiles, cot, self_t, neigh_t
    )
    scores = lax.all_to_all(scores, ("zr", "y"), 0, 0, tiled=True)
    hidden, keep_head, send_head = lax.optimization_barrier((hidden, keep_head, send_head))
    keep_head = keep_head + swap(send_head, "core")
    keep, send = grad(place, hidden, dhidden, feats)
    keep = keep + swap(send, "core")
    keep, scores, keep_head = lax.optimization_barrier((keep, scores, keep_head))
    keep = lax.all_to_all(keep, ("zr", "y"), 0, 0, tiled=True)
    scores = total(scores)
    scores = [scores] + [shift(scores, "zq", s) for s in (1, 2, 3)]
    keep, scores = lax.optimization_barrier((keep, scores))
    keep = sum_x(jnp.concatenate([keep.reshape(-1, TILE), keep_head], axis=0))
    results = finish(place, keep, swap(keep, "core"), deep, classes)
    return (join(place, scores, classes), *results[:4], results[4].reshape(-1))


def solution(mesh):
    split = Mesh(mesh.devices.reshape(4, 2, 4, 2, 4), DP + FEAT)
    return jax.shard_map(
        shards,
        mesh=split,
        in_specs=(
            P(FEAT, None),
            P(DP),
            P(DP, None),
            P(DP, None, None, None),
            P(DP, None),
            P(DP, None, None, None),
            P(FEAT, None),
            P(FEAT, None),
            P(FEAT),
            P(FEAT, None),
            P(FEAT, None),
            P(),
            P(None, DP),
        ),
        out_specs=(
            P(None, DP),
            P(FEAT, None),
            P(FEAT, None),
            P(FEAT, None),
            P(FEAT, None),
            P(FEAT),
        ),
        check_vma=False,
    )
```

```python
import jax
import jax.numpy as jnp
from jax import lax
from jax.experimental import pallas as pl
from jax.experimental.pallas import tpu as pltpu
from jax.sharding import Mesh, PartitionSpec as P

TILE = 128
FEAT = ("zq", "zr", "y")
DP = ("x", "core")
BF = jnp.bfloat16
F32 = jnp.float32
NT = (((1,), (1,)), ((), ()))
VMEM = pl.BlockSpec(memory_space=pltpu.VMEM)
SMEM = pl.BlockSpec(memory_space=pltpu.SMEM)
HBM = pl.BlockSpec(memory_space=pl.ANY)
LIMIT = pltpu.CompilerParams(vmem_limit_bytes=56 * 2**20)


def aligned(index, size):
    return pl.ds(pl.multiple_of(index * size, size), size)


def split_bias(bias):
    row = lax.broadcasted_iota(jnp.int32, (8, bias.shape[1]), 0)
    left = jnp.broadcast_to(bias, row.shape)
    high = left.astype(BF).astype(F32)
    left = left - high
    middle = left.astype(BF).astype(F32)
    low = left - middle
    return jnp.where(row == 0, high, jnp.where(row == 1, middle, jnp.where(row == 2, low, 0.0)))


def hop_kernel(place, ids, cols, table, bias, tiles_hbm, _, out, feats, rows, picked, tiles, sem):
    width = table.shape[0]
    blocks = tiles.shape[0]
    group = blocks // 8
    copies = [
        pltpu.make_async_copy(
            tiles_hbm.at[pl.ds(j * group, group)], tiles.at[pl.ds(j * group, group)], sem.at[j]
        )
        for j in range(8)
    ]
    for copy in copies:
        copy.start()

    def turn(b, carry):
        rows[aligned(b, TILE), 0:width] = table[:, aligned(b, TILE)].astype(F32).T
        return carry

    lax.fori_loop(0, table.shape[1] // TILE, turn, 0, unroll=8)
    step = 64

    def pick(g, carry):
        base = pl.multiple_of(g * step, step)
        for u in range(step):
            picked[pl.ds(base + u, 1), :] = rows[pl.ds(ids[base + u], 1), :]
        return carry

    lax.fori_loop(0, ids.shape[0] // step, pick, 0)
    lane = lax.broadcasted_iota(jnp.int32, (8, TILE), 1)
    term = split_bias(jnp.concatenate([bias[...]] * 4, axis=1))
    term = jnp.where(lane // 32 == place[4], term, 0.0)
    for copy in copies:
        copy.wait()

    def merge(r, carry):
        own = picked[aligned(r, TILE), :].T[0:width]
        left = jnp.concatenate([tiles[r, k] for k in range(8)], axis=1)
        right = jnp.concatenate(
            [picked[aligned(cols[r, k], TILE), :].astype(BF) for k in range(8)], axis=0
        )
        total = jnp.dot(left, right, preferred_element_type=F32)
        both = jnp.concatenate([own, total.T[0:width]], axis=0)
        feats[r] = both.astype(BF)
        out[r] = jnp.concatenate([both, term], axis=0).astype(BF)
        return carry

    lax.fori_loop(0, blocks, merge, 0, unroll=2)


def hop(place, table, ids, cols, bias, tiles, after):
    blocks, deep = tiles.shape[0], 2 * table.shape[0]
    return pl.pallas_call(
        hop_kernel,
        in_specs=[SMEM, SMEM, SMEM, VMEM, VMEM, HBM, HBM],
        out_specs=[VMEM, VMEM],
        scratch_shapes=[
            pltpu.VMEM((table.shape[1], TILE), F32),
            pltpu.VMEM((ids.shape[0], TILE), F32),
            pltpu.VMEM(tiles.shape, BF),
            pltpu.SemaphoreType.DMA((8,)),
        ],
        out_shape=[
            jax.ShapeDtypeStruct((blocks, deep + 8, TILE), BF),
            jax.ShapeDtypeStruct((blocks, deep, TILE), BF),
        ],
        compiler_params=LIMIT,
        cost_estimate=pl.CostEstimate(flops=10**9, bytes_accessed=60 * 10**6, transcendentals=0),
    )(place, ids, cols, table, bias.reshape(1, -1), tiles, after)


def pack_kernel(place, own, neigh, head_self, head_neigh, weights, heads):
    core, x = place[0], place[1]
    cols = aligned(lax.rem(x, 2), 512)
    block = jnp.where(core == 0, own[:, cols].astype(F32), neigh[:, cols].astype(F32)).astype(BF)
    for d in range(weights.shape[0]):
        weights[d] = block
    classes = head_self.shape[1]
    heads[...] = jnp.zeros_like(heads)
    heads[0:32, 0:classes] = head_self[...]
    heads[32:64, 0:classes] = head_neigh[...]


def pack(place, own, neigh, head_self, head_neigh):
    return pl.pallas_call(
        pack_kernel,
        in_specs=[SMEM] + [VMEM] * 4,
        out_specs=[VMEM, VMEM],
        out_shape=[
            jax.ShapeDtypeStruct((32, own.shape[0], 512), BF),
            jax.ShapeDtypeStruct((64, 256), BF),
        ],
        compiler_params=LIMIT,
    )(place, own, neigh, head_self, head_neigh)


def spread_kernel(
    place, cols, live, logit_cot, p0, p1, p2, p3, tiles, out, cot, self_t, neigh_t, own, neigh
):
    classes, slots = logit_cot.shape
    lane = lax.broadcasted_iota(jnp.int32, (classes, slots), 1)
    kept = jnp.where(lane < live[0], logit_cot[...].astype(F32), 0.0)
    cot[...] = jnp.concatenate([kept, jnp.zeros((256 - classes, slots), F32)], axis=0).astype(BF)
    out[...] = jnp.zeros_like(out)
    for s, part in enumerate((p0, p1, p2, p3)):
        at = aligned(lax.rem(place[2] + 4 - s, 4), 32)
        own[at, :] = part[0:32]
        neigh[at, :] = part[32:64]
    self_t[...] = own[...].astype(F32).T.astype(BF)
    neigh_t[...] = neigh[...].astype(F32).T.astype(BF)
    for r in range(tiles.shape[0]):
        part = cot[:, r * TILE : (r + 1) * TILE]
        out[r] = jnp.dot(own[...], part, preferred_element_type=F32)
    for r in range(tiles.shape[0]):
        part = cot[:, r * TILE : (r + 1) * TILE]
        back = jnp.dot(neigh[...], part, preferred_element_type=F32).astype(BF)
        for k in range(8):
            out[cols[r, k]] += jnp.dot(back, tiles[r, k], preferred_element_type=F32)


def spread(place, cols, live, logit_cot, pairs, tiles, blocks):
    return pl.pallas_call(
        spread_kernel,
        in_specs=[SMEM, SMEM, SMEM] + [VMEM] * 6,
        out_specs=[VMEM] * 4,
        scratch_shapes=[pltpu.VMEM((TILE, 256), BF)] * 2,
        out_shape=[
            jax.ShapeDtypeStruct((blocks, TILE, TILE), F32),
            jax.ShapeDtypeStruct((256, logit_cot.shape[1]), BF),
            jax.ShapeDtypeStruct((256, TILE), BF),
            jax.ShapeDtypeStruct((256, TILE), BF),
        ],
        compiler_params=LIMIT,
        cost_estimate=pl.CostEstimate(flops=10**9, bytes_accessed=8 * 10**6, transcendentals=0),
    )(place, cols, live.reshape(1), logit_cot, *pairs, tiles)


def layer_kernel(place, got, w0, w1, w2, o0, o1, o2, out, mine, other):
    core, x = place[0], place[1]
    deep = w0.shape[0] // 32
    for j in range(8):
        pieces = [got[4 * j + i].astype(F32) for i in range(4)]
        own = jnp.concatenate([piece[0:deep] for piece in pieces], axis=0).T.astype(BF)
        agg = jnp.concatenate([piece[deep : 2 * deep] for piece in pieces], axis=0).T.astype(BF)
        at = slice(j * 4 * deep, (j + 1) * 4 * deep)
        mine[:, at] = jnp.where(core == 0, own, agg)
        other[:, at] = jnp.where(core == 0, agg, own)

    def emit(chunk, w, o):
        preact = jnp.dot(mine[...], w, preferred_element_type=F32)
        preact = preact + jnp.dot(other[...], o, preferred_element_type=F32)
        rows = aligned(chunk, 32)
        for half in range(2):
            z = 2 * chunk + half
            terms = sum(got[4 * z + i].astype(F32)[2 * deep :] for i in range(4))
            bias = jnp.sum(terms, axis=0, keepdims=True)
            hidden = jnp.maximum(preact[:, half * TILE : (half + 1) * TILE] + bias, 0.0)
            hidden = hidden.T.astype(BF)
            for y in range(4):
                for zq in range(4):
                    out[8 * zq + 4 * half + y, rows, :] = hidden[32 * y : 32 * y + 32]

    near = 2 * lax.rem(x, 2)
    far = 2 - near
    emit(near, w0[:, 0:256], o0[:, 0:256])
    emit(near + 1, w0[:, 256:512], o0[:, 256:512])
    emit(far, w1[...], o1[...])
    emit(far + 1, w2[...], o2[...])


def layer(place, got, mine, other):
    return pl.pallas_call(
        layer_kernel,
        in_specs=[SMEM] + [VMEM] * 7,
        out_specs=VMEM,
        scratch_shapes=[pltpu.VMEM((TILE, mine[0].shape[0]), BF)] * 2,
        out_shape=jax.ShapeDtypeStruct((32, TILE, TILE), BF),
        compiler_params=LIMIT,
    )(place, got, *mine, *other)


def score_kernel(
    place, cols, hidden, dhidden, tiles, cot, self_t, neigh_t, out, keep, send, second
):
    core, zq = place[0], place[2]
    own = aligned(zq, 32)
    for r in range(tiles.shape[0]):
        left = jnp.concatenate([hidden[cols[r, k]] for k in range(8)], axis=1)
        right = jnp.concatenate([tiles[r, k] for k in range(8)], axis=1)
        second[r] = lax.dot_general(left, right, NT, preferred_element_type=F32).astype(BF)
    halves = []
    for half in range(2):
        at = 2 * zq + half
        scores = jnp.dot(self_t[...], hidden[at], preferred_element_type=F32)
        halves.append(scores + jnp.dot(neigh_t[...], second[at], preferred_element_type=F32))
    block = jnp.concatenate(halves, axis=1)[0 : out.shape[1]].astype(BF)
    for z in range(out.shape[0]):
        out[z] = block
    total = jnp.zeros((32, TILE), F32)
    for b in range(hidden.shape[0]):
        total = total + jnp.where(hidden[b, own, :].astype(F32) > 0.0, dhidden[b, own, :], 0.0)
    mine = jnp.sum(total, axis=1, keepdims=True)
    targets = jnp.concatenate([hidden[r, own, :] for r in range(tiles.shape[0])], axis=1)
    merged = jnp.concatenate([second[r, own, :] for r in range(tiles.shape[0])], axis=1)
    lane = lax.broadcasted_iota(jnp.int32, (32, 256), 1)
    first = lax.dot_general(targets, cot[...], NT, preferred_element_type=F32)
    first = jnp.where(lane == 255, mine, first)
    later = lax.dot_general(merged, cot[...], NT, preferred_element_type=F32)
    kept = jnp.where(core == 0, first, later)
    sent = jnp.where(core == 0, later, first)
    for half in range(2):
        keep[32 * half : 32 * half + 32, :] = kept[:, half * TILE : (half + 1) * TILE]
        send[32 * half : 32 * half + 32, :] = sent[:, half * TILE : (half + 1) * TILE]


def score(place, cols, hidden, dhidden, tiles, cot, self_t, neigh_t):
    shape = jax.ShapeDtypeStruct((64, TILE), F32)
    return pl.pallas_call(
        score_kernel,
        in_specs=[SMEM, SMEM] + [VMEM] * 6,
        out_specs=[VMEM] * 3,
        scratch_shapes=[pltpu.VMEM((tiles.shape[0], TILE, TILE), BF)],
        out_shape=[jax.ShapeDtypeStruct((8, 160, 256), BF), shape, shape],
        compiler_params=LIMIT,
    )(place, cols, hidden, dhidden, tiles, cot, self_t, neigh_t)


def total_kernel(parts, out):
    total = parts[0].astype(F32)
    for j in range(1, parts.shape[0]):
        total = total + parts[j].astype(F32)
    for d in range(out.shape[0]):
        out[d] = total.astype(BF)


def total(parts):
    return pl.pallas_call(
        total_kernel,
        in_specs=[VMEM],
        out_specs=VMEM,
        out_shape=jax.ShapeDtypeStruct((4,) + parts.shape[1:], BF),
        compiler_params=LIMIT,
    )(parts)


def logit_kernel(parts, out):
    classes = out.shape[0]
    for j in range(parts.shape[0]):
        out[:, 256 * j : 256 * (j + 1)] = parts[j].astype(F32)[0:classes]


def join(parts, classes):
    return pl.pallas_call(
        logit_kernel,
        in_specs=[VMEM],
        out_specs=VMEM,
        out_shape=jax.ShapeDtypeStruct((classes, 4 * parts.shape[2]), F32),
        compiler_params=LIMIT,
    )(parts)


def grad_kernel(
    place, hidden, dhidden, f0, f1, f2, e2, f3, g0, g1, g2, d2, g3, keep, send, total
):
    core, zr, y = place[0], place[3], place[4]
    blocks, deep, _ = f0.shape
    half = deep // 2
    total[...] = jnp.zeros_like(total)

    for side in range(2):
        first = side * (blocks // 2)
        far, twin = ((f2, g2), (e2, d2))[side]

        def grow(i, carry):
            b = first + i
            low = jnp.where(hidden[b].astype(F32) > 0.0, dhidden[b], 0.0).astype(BF)
            parts = [f0[b], f1[b], far[i], f3[b], g0[b], g1[b], twin[i], g3[b]]
            stack = jnp.concatenate(parts, axis=0)
            total[...] += lax.dot_general(stack, low, NT, preferred_element_type=F32)
            return carry

        lax.fori_loop(0, blocks // 2, grow, 0, unroll=4)
    for j in range(8):
        owner = 4 * (zr if j < 4 else 1 - zr) + lax.rem(y + 8 - j, 4)
        keep[owner] = total[pl.ds(pl.multiple_of(j * deep + core * half, 8), half), :]
        send[owner] = total[pl.ds(pl.multiple_of(j * deep + (1 - core) * half, 8), half), :]


def grad(place, hidden, dhidden, feats):
    _, deep, _ = feats[0].shape
    shape = jax.ShapeDtypeStruct((8, deep // 2, TILE), F32)
    return pl.pallas_call(
        grad_kernel,
        in_specs=[SMEM] + [VMEM] * 12,
        out_specs=[VMEM, VMEM],
        scratch_shapes=[pltpu.VMEM((8 * deep, TILE), F32)],
        out_shape=[shape, shape],
        compiler_params=LIMIT,
        cost_estimate=pl.CostEstimate(flops=10**9, bytes_accessed=7 * 10**6, transcendentals=0),
    )(place, hidden, dhidden, *feats)


def finish_kernel(place, keep, rest, grad_self, grad_neigh, head_self, head_neigh, bias):
    core = place[0]
    deep = grad_self.shape[0]
    classes = head_self.shape[1]
    first = jnp.where(core == 0, keep[...], rest[...])
    later = jnp.where(core == 0, rest[...], keep[...])
    for value, weight, head in ((first, grad_self, head_self), (later, grad_neigh, head_neigh)):
        for zq in range(4):
            for zr in range(2):
                pieces = [
                    value[(4 * zr + y) * deep : (4 * zr + y + 1) * deep, 32 * zq : 32 * zq + 32]
                    for y in range(4)
                ]
                at = (2 * zq + zr) * TILE
                weight[:, at : at + TILE] = jnp.concatenate(pieces, axis=1)
        base = 8 * deep
        head[:, 0:TILE] = value[base : base + 32]
        head[:, TILE:classes] = value[base + 32 : base + 64, 0 : classes - TILE]
    bias[...] = first[8 * deep + 32 : 8 * deep + 64].T[TILE - 1 : TILE]


def finish(place, keep, rest, deep, classes):
    weight = jax.ShapeDtypeStruct((deep, 1024), F32)
    head = jax.ShapeDtypeStruct((32, classes), F32)
    return pl.pallas_call(
        finish_kernel,
        in_specs=[SMEM, VMEM, VMEM],
        out_specs=[VMEM] * 5,
        out_shape=[weight, weight, head, head, jax.ShapeDtypeStruct((1, 32), F32)],
        compiler_params=LIMIT,
    )(place, keep, rest)


def shift(value, axis, by):
    return lax.ppermute(value, axis, [(i, (i + by) % 4) for i in range(4)])


def relay(value, near):
    half = value.shape[0] // 2
    far = [shift(near[0][:half], "y", 1), shift(near[1][half:], "y", 3)]
    return [value, near[0], *far, near[1]]


def swap(value, axis):
    return lax.ppermute(value, axis, [(0, 1), (1, 0)])


def sum_x(value):
    value = value + lax.ppermute(value, "x", [(0, 1), (1, 0), (2, 3), (3, 2)])
    return value + lax.ppermute(value, "x", [(0, 3), (3, 0), (1, 2), (2, 1)])


def shards(
    feature_table,
    node_ids,
    hop_cols,
    hop_tiles,
    target_cols,
    target_tiles,
    self_weight,
    neigh_weight,
    hidden_bias,
    head_self,
    head_neigh,
    batch_sizes,
    logit_cotangent,
):
    blocks = hop_cols.shape[0]
    deep = feature_table.shape[0]
    classes, target_rows = logit_cotangent.shape
    place = jnp.stack([lax.axis_index(axis) for axis in ("core", "x") + FEAT])

    packed, pair = pack(place, self_weight, neigh_weight, head_self, head_neigh)
    weights = lax.all_to_all(packed, FEAT, 0, 0, tiled=True)
    send, feats = hop(
        place, feature_table, node_ids, hop_cols, hidden_bias, hop_tiles, packed
    )
    weights, pair, send, feats = lax.optimization_barrier((weights, pair, send, feats))
    got = lax.all_to_all(send, FEAT, 0, 0, tiled=True)
    weights = weights.reshape(-1, 512)
    mine = [weights, shift(weights[:, :256], "x", 1), shift(weights[:, 256:], "x", 3)]
    other = [swap(w, "core") for w in mine]

    twin = swap(feats, "zr")
    near = [shift(feats, "y", s) for s in (1, 3)]
    pairs = [pair] + [shift(pair, "zq", s) for s in (1, 2, 3)]

    hidden = layer(place, got, mine, other)
    hidden, pairs, near, feats, twin = lax.optimization_barrier(
        (hidden, pairs, near, feats, twin)
    )
    hidden = lax.all_to_all(hidden, FEAT, 0, 0, tiled=True)
    feats = relay(feats, near) + relay(twin, [shift(twin, "y", s) for s in (1, 3)])
    live = batch_sizes[lax.axis_index("x") * 2 + lax.axis_index("core")]
    dhidden, cot, self_t, neigh_t = spread(
        place, target_cols, live, logit_cotangent, pairs, target_tiles, blocks
    )
    hidden, feats = lax.optimization_barrier((hidden, feats))

    scores, keep_head, send_head = score(
        place, target_cols, hidden, dhidden, target_tiles, cot, self_t, neigh_t
    )
    scores = lax.all_to_all(scores, ("zr", "y"), 0, 0, tiled=True)
    hidden, keep_head, send_head = lax.optimization_barrier((hidden, keep_head, send_head))
    keep_head = keep_head + swap(send_head, "core")
    keep, send = grad(place, hidden, dhidden, feats)
    keep = keep + swap(send, "core")
    keep, scores, keep_head = lax.optimization_barrier((keep, scores, keep_head))
    keep = lax.all_to_all(keep, ("zr", "y"), 0, 0, tiled=True)
    keep, scores = lax.optimization_barrier((keep, total(scores)))
    scores = lax.all_to_all(scores, "zq", 0, 0, tiled=True)
    keep = sum_x(jnp.concatenate([keep.reshape(-1, TILE), keep_head], axis=0))
    results = finish(place, keep, swap(keep, "core"), deep, classes)
    return (join(scores, classes), *results[:4], results[4].reshape(-1))


def solution(mesh):
    split = Mesh(mesh.devices.reshape(4, 2, 4, 2, 4), DP + FEAT)
    return jax.shard_map(
        shards,
        mesh=split,
        in_specs=(
            P(FEAT, None),
            P(DP),
            P(DP, None),
            P(DP, None, None, None),
            P(DP, None),
            P(DP, None, None, None),
            P(FEAT, None),
            P(FEAT, None),
            P(FEAT),
            P(FEAT, None),
            P(FEAT, None),
            P(),
            P(None, DP),
        ),
        out_specs=(
            P(None, DP),
            P(FEAT, None),
            P(FEAT, None),
            P(FEAT, None),
            P(FEAT, None),
            P(FEAT),
        ),
        check_vma=False,
    )
```

```python
import jax
import jax.numpy as jnp
from jax import lax
from jax.experimental import pallas as pl
from jax.experimental.pallas import tpu as pltpu
from jax.sharding import Mesh, PartitionSpec as P

TILE = 128
FEAT = ("zq", "zr", "y")
DP = ("x", "core")
BF = jnp.bfloat16
F32 = jnp.float32
NT = (((1,), (1,)), ((), ()))
VMEM = pl.BlockSpec(memory_space=pltpu.VMEM)
SMEM = pl.BlockSpec(memory_space=pltpu.SMEM)
HBM = pl.BlockSpec(memory_space=pl.ANY)
LIMIT = pltpu.CompilerParams(vmem_limit_bytes=56 * 2**20)


def aligned(index, size):
    return pl.ds(pl.multiple_of(index * size, size), size)


def split_bias(bias):
    row = lax.broadcasted_iota(jnp.int32, (8, bias.shape[1]), 0)
    left = jnp.broadcast_to(bias, row.shape)
    high = left.astype(BF).astype(F32)
    left = left - high
    middle = left.astype(BF).astype(F32)
    low = left - middle
    return jnp.where(row == 0, high, jnp.where(row == 1, middle, jnp.where(row == 2, low, 0.0)))


def hop_kernel(place, ids, cols, table, bias, tiles_hbm, _, out, feats, rows, picked, tiles, sem):
    width = table.shape[0]
    blocks = tiles.shape[0]
    group = blocks // 8
    copies = [
        pltpu.make_async_copy(
            tiles_hbm.at[pl.ds(j * group, group)], tiles.at[pl.ds(j * group, group)], sem.at[j]
        )
        for j in range(8)
    ]
    for copy in copies:
        copy.start()

    def turn(b, carry):
        rows[aligned(b, TILE), 0:width] = table[:, aligned(b, TILE)].astype(F32).T
        return carry

    lax.fori_loop(0, table.shape[1] // TILE, turn, 0, unroll=8)
    step = 64

    def pick(g, carry):
        base = pl.multiple_of(g * step, step)
        for u in range(step):
            picked[pl.ds(base + u, 1), :] = rows[pl.ds(ids[base + u], 1), :]
        return carry

    lax.fori_loop(0, ids.shape[0] // step, pick, 0)
    lane = lax.broadcasted_iota(jnp.int32, (8, TILE), 1)
    term = split_bias(jnp.concatenate([bias[...]] * 4, axis=1))
    term = jnp.where(lane // 32 == place[4], term, 0.0)
    for copy in copies:
        copy.wait()

    def merge(r, carry):
        own = picked[aligned(r, TILE), :].T[0:width]
        left = jnp.concatenate([tiles[r, k] for k in range(8)], axis=1)
        right = jnp.concatenate(
            [picked[aligned(cols[r, k], TILE), :].astype(BF) for k in range(8)], axis=0
        )
        total = jnp.dot(left, right, preferred_element_type=F32)
        both = jnp.concatenate([own, total.T[0:width]], axis=0)
        feats[r] = both.astype(BF)
        out[r] = jnp.concatenate([both, term], axis=0).astype(BF)
        return carry

    lax.fori_loop(0, blocks, merge, 0, unroll=2)


def hop(place, table, ids, cols, bias, tiles, after):
    blocks, deep = tiles.shape[0], 2 * table.shape[0]
    return pl.pallas_call(
        hop_kernel,
        in_specs=[SMEM, SMEM, SMEM, VMEM, VMEM, HBM, HBM],
        out_specs=[VMEM, VMEM],
        scratch_shapes=[
            pltpu.VMEM((table.shape[1], TILE), F32),
            pltpu.VMEM((ids.shape[0], TILE), F32),
            pltpu.VMEM(tiles.shape, BF),
            pltpu.SemaphoreType.DMA((8,)),
        ],
        out_shape=[
            jax.ShapeDtypeStruct((blocks, deep + 8, TILE), BF),
            jax.ShapeDtypeStruct((blocks, deep, TILE), BF),
        ],
        compiler_params=LIMIT,
        cost_estimate=pl.CostEstimate(flops=10**9, bytes_accessed=60 * 10**6, transcendentals=0),
    )(place, ids, cols, table, bias.reshape(1, -1), tiles, after)


def pack_kernel(place, own, neigh, head_self, head_neigh, weights, heads):
    core, x = place[0], place[1]
    cols = aligned(lax.rem(x, 2), 512)
    block = jnp.where(core == 0, own[:, cols].astype(F32), neigh[:, cols].astype(F32)).astype(BF)
    for d in range(weights.shape[0]):
        weights[d] = block
    classes = head_self.shape[1]
    heads[...] = jnp.zeros_like(heads)
    heads[0:32, 0:classes] = head_self[...]
    heads[32:64, 0:classes] = head_neigh[...]


def pack(place, own, neigh, head_self, head_neigh):
    return pl.pallas_call(
        pack_kernel,
        in_specs=[SMEM] + [VMEM] * 4,
        out_specs=[VMEM, VMEM],
        out_shape=[
            jax.ShapeDtypeStruct((32, own.shape[0], 512), BF),
            jax.ShapeDtypeStruct((64, 256), BF),
        ],
        compiler_params=LIMIT,
    )(place, own, neigh, head_self, head_neigh)


def spread_kernel(
    place, cols, live, logit_cot, pair, quad, tiles, out, cot, self_t, neigh_t, own, neigh
):
    classes, slots = logit_cot.shape
    lane = lax.broadcasted_iota(jnp.int32, (classes, slots), 1)
    kept = jnp.where(lane < live[0], logit_cot[...].astype(F32), 0.0)
    cot[...] = jnp.concatenate([kept, jnp.zeros((256 - classes, slots), F32)], axis=0).astype(BF)
    out[...] = jnp.zeros_like(out)
    zq = place[2]
    low, high = 2 * (zq // 2), 2 - 2 * (zq // 2)
    odd = lax.rem(zq, 2)
    for part, first in ((pair, low), (quad, high)):
        for j, at in enumerate((first + odd, first + 1 - odd)):
            own[aligned(at, 32), :] = part[64 * j : 64 * j + 32]
            neigh[aligned(at, 32), :] = part[64 * j + 32 : 64 * j + 64]
    self_t[...] = own[...].astype(F32).T.astype(BF)
    neigh_t[...] = neigh[...].astype(F32).T.astype(BF)
    for r in range(tiles.shape[0]):
        part = cot[:, r * TILE : (r + 1) * TILE]
        out[r] = jnp.dot(own[...], part, preferred_element_type=F32)
    for r in range(tiles.shape[0]):
        part = cot[:, r * TILE : (r + 1) * TILE]
        back = jnp.dot(neigh[...], part, preferred_element_type=F32).astype(BF)
        for k in range(8):
            out[cols[r, k]] += jnp.dot(back, tiles[r, k], preferred_element_type=F32)


def spread(place, cols, live, logit_cot, pair, quad, tiles, blocks):
    return pl.pallas_call(
        spread_kernel,
        in_specs=[SMEM, SMEM, SMEM] + [VMEM] * 4,
        out_specs=[VMEM] * 4,
        scratch_shapes=[pltpu.VMEM((TILE, 256), BF)] * 2,
        out_shape=[
            jax.ShapeDtypeStruct((blocks, TILE, TILE), F32),
            jax.ShapeDtypeStruct((256, logit_cot.shape[1]), BF),
            jax.ShapeDtypeStruct((256, TILE), BF),
            jax.ShapeDtypeStruct((256, TILE), BF),
        ],
        compiler_params=LIMIT,
        cost_estimate=pl.CostEstimate(flops=10**9, bytes_accessed=8 * 10**6, transcendentals=0),
    )(place, cols, live.reshape(1), logit_cot, pair, quad, tiles)


def layer_kernel(place, got, w0, w1, w2, o0, o1, o2, out, mine, other):
    core, x = place[0], place[1]
    deep = w0.shape[0] // 32
    for j in range(8):
        pieces = [got[4 * j + i].astype(F32) for i in range(4)]
        own = jnp.concatenate([piece[0:deep] for piece in pieces], axis=0).T.astype(BF)
        agg = jnp.concatenate([piece[deep : 2 * deep] for piece in pieces], axis=0).T.astype(BF)
        at = slice(j * 4 * deep, (j + 1) * 4 * deep)
        mine[:, at] = jnp.where(core == 0, own, agg)
        other[:, at] = jnp.where(core == 0, agg, own)

    def emit(chunk, w, o):
        preact = jnp.dot(mine[...], w, preferred_element_type=F32)
        preact = preact + jnp.dot(other[...], o, preferred_element_type=F32)
        rows = aligned(chunk, 32)
        for half in range(2):
            z = 2 * chunk + half
            terms = sum(got[4 * z + i].astype(F32)[2 * deep :] for i in range(4))
            bias = jnp.sum(terms, axis=0, keepdims=True)
            hidden = jnp.maximum(preact[:, half * TILE : (half + 1) * TILE] + bias, 0.0)
            hidden = hidden.T.astype(BF)
            for y in range(4):
                for zq in range(4):
                    out[8 * zq + 4 * half + y, rows, :] = hidden[32 * y : 32 * y + 32]

    near = 2 * lax.rem(x, 2)
    far = 2 - near
    emit(near, w0[:, 0:256], o0[:, 0:256])
    emit(near + 1, w0[:, 256:512], o0[:, 256:512])
    emit(far, w1[...], o1[...])
    emit(far + 1, w2[...], o2[...])


def layer(place, got, mine, other):
    return pl.pallas_call(
        layer_kernel,
        in_specs=[SMEM] + [VMEM] * 7,
        out_specs=VMEM,
        scratch_shapes=[pltpu.VMEM((TILE, mine[0].shape[0]), BF)] * 2,
        out_shape=jax.ShapeDtypeStruct((32, TILE, TILE), BF),
        compiler_params=LIMIT,
    )(place, got, *mine, *other)


def score_kernel(
    place, cols, hidden, dhidden, tiles, cot, self_t, neigh_t, out, keep, send, second
):
    core, zq = place[0], place[2]
    own = aligned(zq, 32)
    for r in range(tiles.shape[0]):
        left = jnp.concatenate([hidden[cols[r, k]] for k in range(8)], axis=1)
        right = jnp.concatenate([tiles[r, k] for k in range(8)], axis=1)
        second[r] = lax.dot_general(left, right, NT, preferred_element_type=F32).astype(BF)
    halves = []
    for half in range(2):
        at = 2 * zq + half
        scores = jnp.dot(self_t[...], hidden[at], preferred_element_type=F32)
        halves.append(scores + jnp.dot(neigh_t[...], second[at], preferred_element_type=F32))
    block = jnp.concatenate(halves, axis=1)[0 : out.shape[1]].astype(BF)
    for z in range(out.shape[0]):
        out[z] = block
    total = jnp.zeros((32, TILE), F32)
    for b in range(hidden.shape[0]):
        total = total + jnp.where(hidden[b, own, :].astype(F32) > 0.0, dhidden[b, own, :], 0.0)
    mine = jnp.sum(total, axis=1, keepdims=True)
    targets = jnp.concatenate([hidden[r, own, :] for r in range(tiles.shape[0])], axis=1)
    merged = jnp.concatenate([second[r, own, :] for r in range(tiles.shape[0])], axis=1)
    lane = lax.broadcasted_iota(jnp.int32, (32, 256), 1)
    first = lax.dot_general(targets, cot[...], NT, preferred_element_type=F32)
    first = jnp.where(lane == 255, mine, first)
    later = lax.dot_general(merged, cot[...], NT, preferred_element_type=F32)
    kept = jnp.where(core == 0, first, later)
    sent = jnp.where(core == 0, later, first)
    for half in range(2):
        keep[32 * half : 32 * half + 32, :] = kept[:, half * TILE : (half + 1) * TILE]
        send[32 * half : 32 * half + 32, :] = sent[:, half * TILE : (half + 1) * TILE]


def score(place, cols, hidden, dhidden, tiles, cot, self_t, neigh_t):
    shape = jax.ShapeDtypeStruct((64, TILE), F32)
    return pl.pallas_call(
        score_kernel,
        in_specs=[SMEM, SMEM] + [VMEM] * 6,
        out_specs=[VMEM] * 3,
        scratch_shapes=[pltpu.VMEM((tiles.shape[0], TILE, TILE), BF)],
        out_shape=[jax.ShapeDtypeStruct((8, 160, 256), BF), shape, shape],
        compiler_params=LIMIT,
    )(place, cols, hidden, dhidden, tiles, cot, self_t, neigh_t)


def total_kernel(parts, out):
    total = parts[0].astype(F32)
    for j in range(1, parts.shape[0]):
        total = total + parts[j].astype(F32)
    for d in range(out.shape[0]):
        out[d] = total.astype(BF)


def total(parts):
    return pl.pallas_call(
        total_kernel,
        in_specs=[VMEM],
        out_specs=VMEM,
        out_shape=jax.ShapeDtypeStruct((4,) + parts.shape[1:], BF),
        compiler_params=LIMIT,
    )(parts)


def logit_kernel(parts, out):
    classes = out.shape[0]
    for j in range(parts.shape[0]):
        out[:, 256 * j : 256 * (j + 1)] = parts[j].astype(F32)[0:classes]


def join(parts, classes):
    return pl.pallas_call(
        logit_kernel,
        in_specs=[VMEM],
        out_specs=VMEM,
        out_shape=jax.ShapeDtypeStruct((classes, 4 * parts.shape[2]), F32),
        compiler_params=LIMIT,
    )(parts)


def grad_kernel(
    place, hidden, dhidden, f0, f1, f2, e2, f3, g0, g1, g2, d2, g3, keep, send, total
):
    core, zr, y = place[0], place[3], place[4]
    blocks, deep, _ = f0.shape
    half = deep // 2
    total[...] = jnp.zeros_like(total)

    for side in range(2):
        first = side * (blocks // 2)
        far, twin = ((f2, g2), (e2, d2))[side]

        def grow(i, carry):
            b = first + i
            low = jnp.where(hidden[b].astype(F32) > 0.0, dhidden[b], 0.0).astype(BF)
            parts = [f0[b], f1[b], far[i], f3[b], g0[b], g1[b], twin[i], g3[b]]
            stack = jnp.concatenate(parts, axis=0)
            total[...] += lax.dot_general(stack, low, NT, preferred_element_type=F32)
            return carry

        lax.fori_loop(0, blocks // 2, grow, 0, unroll=4)
    for j in range(8):
        owner = 4 * (zr if j < 4 else 1 - zr) + lax.rem(y + 8 - j, 4)
        keep[owner] = total[pl.ds(pl.multiple_of(j * deep + core * half, 8), half), :]
        send[owner] = total[pl.ds(pl.multiple_of(j * deep + (1 - core) * half, 8), half), :]


def grad(place, hidden, dhidden, feats):
    _, deep, _ = feats[0].shape
    shape = jax.ShapeDtypeStruct((8, deep // 2, TILE), F32)
    return pl.pallas_call(
        grad_kernel,
        in_specs=[SMEM] + [VMEM] * 12,
        out_specs=[VMEM, VMEM],
        scratch_shapes=[pltpu.VMEM((8 * deep, TILE), F32)],
        out_shape=[shape, shape],
        compiler_params=LIMIT,
        cost_estimate=pl.CostEstimate(flops=10**9, bytes_accessed=7 * 10**6, transcendentals=0),
    )(place, hidden, dhidden, *feats)


def finish_kernel(place, keep, rest, grad_self, grad_neigh, head_self, head_neigh, bias):
    core = place[0]
    deep = grad_self.shape[0]
    classes = head_self.shape[1]
    first = jnp.where(core == 0, keep[...], rest[...])
    later = jnp.where(core == 0, rest[...], keep[...])
    for value, weight, head in ((first, grad_self, head_self), (later, grad_neigh, head_neigh)):
        for zq in range(4):
            for zr in range(2):
                pieces = [
                    value[(4 * zr + y) * deep : (4 * zr + y + 1) * deep, 32 * zq : 32 * zq + 32]
                    for y in range(4)
                ]
                at = (2 * zq + zr) * TILE
                weight[:, at : at + TILE] = jnp.concatenate(pieces, axis=1)
        base = 8 * deep
        head[:, 0:TILE] = value[base : base + 32]
        head[:, TILE:classes] = value[base + 32 : base + 64, 0 : classes - TILE]
    bias[...] = first[8 * deep + 32 : 8 * deep + 64].T[TILE - 1 : TILE]


def finish(place, keep, rest, deep, classes):
    weight = jax.ShapeDtypeStruct((deep, 1024), F32)
    head = jax.ShapeDtypeStruct((32, classes), F32)
    return pl.pallas_call(
        finish_kernel,
        in_specs=[SMEM, VMEM, VMEM],
        out_specs=[VMEM] * 5,
        out_shape=[weight, weight, head, head, jax.ShapeDtypeStruct((1, 32), F32)],
        compiler_params=LIMIT,
    )(place, keep, rest)


def shift(value, axis, by):
    return lax.ppermute(value, axis, [(i, (i + by) % 4) for i in range(4)])


def relay(value, near):
    half = value.shape[0] // 2
    far = [shift(near[0][:half], "y", 1), shift(near[1][half:], "y", 3)]
    return [value, near[0], *far, near[1]]


def swap(value, axis):
    return lax.ppermute(value, axis, [(0, 1), (1, 0)])


def shards(
    feature_table,
    node_ids,
    hop_cols,
    hop_tiles,
    target_cols,
    target_tiles,
    self_weight,
    neigh_weight,
    hidden_bias,
    head_self,
    head_neigh,
    batch_sizes,
    logit_cotangent,
):
    blocks = hop_cols.shape[0]
    deep = feature_table.shape[0]
    classes, target_rows = logit_cotangent.shape
    place = jnp.stack([lax.axis_index(axis) for axis in ("core", "x") + FEAT])

    packed, pair = pack(place, self_weight, neigh_weight, head_self, head_neigh)
    weights = lax.all_to_all(packed, FEAT, 0, 0, tiled=True)
    send, feats = hop(
        place, feature_table, node_ids, hop_cols, hidden_bias, hop_tiles, packed
    )
    peer = lax.ppermute(pair, "zq", [(0, 1), (1, 0), (2, 3), (3, 2)])
    weights, pair, peer, send, feats = lax.optimization_barrier(
        (weights, pair, peer, send, feats)
    )
    got = lax.all_to_all(send, FEAT, 0, 0, tiled=True)
    weights = weights.reshape(-1, 512)
    mine = [weights, shift(weights[:, :256], "x", 1), shift(weights[:, 256:], "x", 3)]

    mine, feats = lax.optimization_barrier((mine, feats))
    other = [swap(w, "core") for w in mine]
    twin = swap(feats, "zr")
    near = [shift(feats, "y", s) for s in (1, 3)]
    pair = jnp.concatenate([pair, peer], axis=0)
    quad = lax.ppermute(pair, "zq", [(0, 2), (2, 0), (1, 3), (3, 1)])

    hidden = layer(place, got, mine, other)
    hidden, pair, quad, near, feats, twin = lax.optimization_barrier(
        (hidden, pair, quad, near, feats, twin)
    )
    hidden = lax.all_to_all(hidden, FEAT, 0, 0, tiled=True)
    feats = relay(feats, near)
    near = [shift(twin, "y", s) for s in (1, 3)]
    live = batch_sizes[lax.axis_index("x") * 2 + lax.axis_index("core")]
    ready = spread(place, target_cols, live, logit_cotangent, pair, quad, target_tiles, blocks)
    ready, near = lax.optimization_barrier((ready, near))
    dhidden, cot, self_t, neigh_t = ready
    feats = feats + relay(twin, near)
    hidden, feats = lax.optimization_barrier((hidden, feats))

    scores, keep_head, send_head = score(
        place, target_cols, hidden, dhidden, target_tiles, cot, self_t, neigh_t
    )
    scores = lax.all_to_all(scores, ("zr", "y"), 0, 0, tiled=True)
    hidden, keep_head, send_head = lax.optimization_barrier((hidden, keep_head, send_head))
    keep_head = keep_head + swap(send_head, "core")
    keep, send = grad(place, hidden, dhidden, feats)
    keep = keep + swap(send, "core")
    keep, scores, keep_head = lax.optimization_barrier((keep, scores, keep_head))
    keep = lax.all_to_all(keep, ("zr", "y"), 0, 0, tiled=True)
    keep, scores = lax.optimization_barrier((keep, total(scores)))
    keep = jnp.concatenate([keep.reshape(-1, TILE), keep_head], axis=0)
    scores = lax.all_to_all(scores, "zq", 0, 0, tiled=True)
    keep = keep + lax.ppermute(keep, "x", [(0, 1), (1, 0), (2, 3), (3, 2)])
    keep = keep + lax.ppermute(keep, "x", [(0, 3), (3, 0), (1, 2), (2, 1)])
    results = finish(place, keep, swap(keep, "core"), deep, classes)
    return (join(scores, classes), *results[:4], results[4].reshape(-1))


def solution(mesh):
    split = Mesh(mesh.devices.reshape(4, 2, 4, 2, 4), DP + FEAT)
    return jax.shard_map(
        shards,
        mesh=split,
        in_specs=(
            P(FEAT, None),
            P(DP),
            P(DP, None),
            P(DP, None, None, None),
            P(DP, None),
            P(DP, None, None, None),
            P(FEAT, None),
            P(FEAT, None),
            P(FEAT),
            P(FEAT, None),
            P(FEAT, None),
            P(),
            P(None, DP),
        ),
        out_specs=(
            P(None, DP),
            P(FEAT, None),
            P(FEAT, None),
            P(FEAT, None),
            P(FEAT, None),
            P(FEAT),
        ),
        check_vma=False,
    )
```

```python
import jax
import jax.numpy as jnp
from jax import lax
from jax.experimental import pallas as pl
from jax.experimental.pallas import tpu as pltpu
from jax.sharding import Mesh, PartitionSpec as P

TILE = 128
FEAT = ("zq", "zr", "y")
DP = ("x", "core")
BF = jnp.bfloat16
F32 = jnp.float32
NT = (((1,), (1,)), ((), ()))
VMEM = pl.BlockSpec(memory_space=pltpu.VMEM)
SMEM = pl.BlockSpec(memory_space=pltpu.SMEM)
HBM = pl.BlockSpec(memory_space=pl.ANY)
LIMIT = pltpu.CompilerParams(vmem_limit_bytes=56 * 2**20)


def aligned(index, size):
    return pl.ds(pl.multiple_of(index * size, size), size)


def split_bias(bias):
    row = lax.broadcasted_iota(jnp.int32, (8, bias.shape[1]), 0)
    left = jnp.broadcast_to(bias, row.shape)
    high = left.astype(BF).astype(F32)
    left = left - high
    middle = left.astype(BF).astype(F32)
    low = left - middle
    return jnp.where(row == 0, high, jnp.where(row == 1, middle, jnp.where(row == 2, low, 0.0)))


def hop_kernel(place, ids, cols, table, bias, tiles_hbm, _, out, feats, rows, picked, tiles, sem):
    width = table.shape[0]
    blocks = tiles.shape[0]
    group = blocks // 8
    copies = [
        pltpu.make_async_copy(
            tiles_hbm.at[pl.ds(j * group, group)], tiles.at[pl.ds(j * group, group)], sem.at[j]
        )
        for j in range(8)
    ]
    for copy in copies:
        copy.start()

    def turn(b, carry):
        rows[aligned(b, TILE), 0:width] = table[:, aligned(b, TILE)].astype(F32).T
        return carry

    lax.fori_loop(0, table.shape[1] // TILE, turn, 0, unroll=16)
    step = 64

    def pick(g, carry):
        base = pl.multiple_of(g * step, step)
        for u in range(step):
            picked[pl.ds(base + u, 1), :] = rows[pl.ds(ids[base + u], 1), :]
        return carry

    lax.fori_loop(0, ids.shape[0] // step, pick, 0)
    lane = lax.broadcasted_iota(jnp.int32, (8, TILE), 1)
    term = split_bias(jnp.concatenate([bias[...]] * 4, axis=1))
    term = jnp.where(lane // 32 == place[4], term, 0.0)
    for copy in copies:
        copy.wait()

    def merge(r, carry):
        own = picked[aligned(r, TILE), :].T[0:width]
        left = jnp.concatenate([tiles[r, k] for k in range(8)], axis=1)
        right = jnp.concatenate(
            [picked[aligned(cols[r, k], TILE), :].astype(BF) for k in range(8)], axis=0
        )
        total = jnp.dot(left, right, preferred_element_type=F32)
        both = jnp.concatenate([own, total.T[0:width]], axis=0)
        feats[r] = both.astype(BF)
        out[r] = jnp.concatenate([both, term], axis=0).astype(BF)
        return carry

    lax.fori_loop(0, blocks, merge, 0, unroll=4)


def hop(place, table, ids, cols, bias, tiles, after):
    blocks, deep = tiles.shape[0], 2 * table.shape[0]
    return pl.pallas_call(
        hop_kernel,
        in_specs=[SMEM, SMEM, SMEM, VMEM, VMEM, HBM, HBM],
        out_specs=[VMEM, VMEM],
        scratch_shapes=[
            pltpu.VMEM((table.shape[1], TILE), F32),
            pltpu.VMEM((ids.shape[0], TILE), F32),
            pltpu.VMEM(tiles.shape, BF),
            pltpu.SemaphoreType.DMA((8,)),
        ],
        out_shape=[
            jax.ShapeDtypeStruct((blocks, deep + 8, TILE), BF),
            jax.ShapeDtypeStruct((blocks, deep, TILE), BF),
        ],
        compiler_params=LIMIT,
        cost_estimate=pl.CostEstimate(flops=10**9, bytes_accessed=60 * 10**6, transcendentals=0),
    )(place, ids, cols, table, bias.reshape(1, -1), tiles, after)


def pack_kernel(place, own, neigh, head_self, head_neigh, weights, heads):
    core, x = place[0], place[1]
    cols = aligned(lax.rem(x, 2), 512)
    block = jnp.where(core == 0, own[:, cols].astype(F32), neigh[:, cols].astype(F32)).astype(BF)
    for d in range(weights.shape[0]):
        weights[d] = block
    classes = head_self.shape[1]
    heads[...] = jnp.zeros_like(heads)
    heads[0:32, 0:classes] = head_self[...]
    heads[32:64, 0:classes] = head_neigh[...]


def pack(place, own, neigh, head_self, head_neigh):
    return pl.pallas_call(
        pack_kernel,
        in_specs=[SMEM] + [VMEM] * 4,
        out_specs=[VMEM, VMEM],
        out_shape=[
            jax.ShapeDtypeStruct((32, own.shape[0], 512), BF),
            jax.ShapeDtypeStruct((64, 256), BF),
        ],
        compiler_params=LIMIT,
    )(place, own, neigh, head_self, head_neigh)


def spread_kernel(
    place, cols, live, logit_cot, pair, quad, tiles, out, cot, self_t, neigh_t, own, neigh
):
    classes, slots = logit_cot.shape
    lane = lax.broadcasted_iota(jnp.int32, (classes, slots), 1)
    kept = jnp.where(lane < live[0], logit_cot[...].astype(F32), 0.0)
    cot[...] = jnp.concatenate([kept, jnp.zeros((256 - classes, slots), F32)], axis=0).astype(BF)
    out[...] = jnp.zeros_like(out)
    zq = place[2]
    side, odd = lax.rem(zq, 2), zq // 2
    for part, first in ((pair, side), (quad, 1 - side)):
        for j, at in enumerate((first + 2 * odd, first + 2 - 2 * odd)):
            own[aligned(at, 32), :] = part[64 * j : 64 * j + 32]
            neigh[aligned(at, 32), :] = part[64 * j + 32 : 64 * j + 64]
    self_t[...] = own[...].astype(F32).T.astype(BF)
    neigh_t[...] = neigh[...].astype(F32).T.astype(BF)
    for r in range(tiles.shape[0]):
        part = cot[:, r * TILE : (r + 1) * TILE]
        out[r] = jnp.dot(own[...], part, preferred_element_type=F32)
    for r in range(tiles.shape[0]):
        part = cot[:, r * TILE : (r + 1) * TILE]
        back = jnp.dot(neigh[...], part, preferred_element_type=F32).astype(BF)
        for k in range(8):
            out[cols[r, k]] += jnp.dot(back, tiles[r, k], preferred_element_type=F32)


def spread(place, cols, live, logit_cot, pair, quad, tiles, blocks):
    return pl.pallas_call(
        spread_kernel,
        in_specs=[SMEM, SMEM, SMEM] + [VMEM] * 4,
        out_specs=[VMEM] * 4,
        scratch_shapes=[pltpu.VMEM((TILE, 256), BF)] * 2,
        out_shape=[
            jax.ShapeDtypeStruct((blocks, TILE, TILE), F32),
            jax.ShapeDtypeStruct((256, logit_cot.shape[1]), BF),
            jax.ShapeDtypeStruct((256, TILE), BF),
            jax.ShapeDtypeStruct((256, TILE), BF),
        ],
        compiler_params=LIMIT,
        cost_estimate=pl.CostEstimate(flops=10**9, bytes_accessed=8 * 10**6, transcendentals=0),
    )(place, cols, live.reshape(1), logit_cot, pair, quad, tiles)


def layer_kernel(place, got, w0, w1, w2, o0, o1, o2, out, mine, other):
    core, x = place[0], place[1]
    deep = w0.shape[0] // 32
    for j in range(8):
        pieces = [got[4 * j + i].astype(F32) for i in range(4)]
        own = jnp.concatenate([piece[0:deep] for piece in pieces], axis=0).T.astype(BF)
        agg = jnp.concatenate([piece[deep : 2 * deep] for piece in pieces], axis=0).T.astype(BF)
        at = slice(j * 4 * deep, (j + 1) * 4 * deep)
        mine[:, at] = jnp.where(core == 0, own, agg)
        other[:, at] = jnp.where(core == 0, agg, own)

    def emit(chunk, w, o):
        preact = jnp.dot(mine[...], w, preferred_element_type=F32)
        preact = preact + jnp.dot(other[...], o, preferred_element_type=F32)
        rows = aligned(chunk, 32)
        for half in range(2):
            z = 2 * chunk + half
            terms = sum(got[4 * z + i].astype(F32)[2 * deep :] for i in range(4))
            bias = jnp.sum(terms, axis=0, keepdims=True)
            hidden = jnp.maximum(preact[:, half * TILE : (half + 1) * TILE] + bias, 0.0)
            hidden = hidden.T.astype(BF)
            for y in range(4):
                for zq in range(4):
                    out[8 * zq + 4 * half + y, rows, :] = hidden[32 * y : 32 * y + 32]

    near = 2 * lax.rem(x, 2)
    far = 2 - near
    emit(near, w0[:, 0:256], o0[:, 0:256])
    emit(near + 1, w0[:, 256:512], o0[:, 256:512])
    emit(far, w1[...], o1[...])
    emit(far + 1, w2[...], o2[...])


def layer(place, got, mine, other):
    return pl.pallas_call(
        layer_kernel,
        in_specs=[SMEM] + [VMEM] * 7,
        out_specs=VMEM,
        scratch_shapes=[pltpu.VMEM((TILE, mine[0].shape[0]), BF)] * 2,
        out_shape=jax.ShapeDtypeStruct((32, TILE, TILE), BF),
        compiler_params=LIMIT,
    )(place, got, *mine, *other)


def score_kernel(
    place, cols, hidden, dhidden, tiles, cot, self_t, neigh_t, out, keep, send, second
):
    core, zq = place[0], place[2]
    own = aligned(zq, 32)
    for r in range(tiles.shape[0]):
        left = jnp.concatenate([hidden[cols[r, k]] for k in range(8)], axis=1)
        right = jnp.concatenate([tiles[r, k] for k in range(8)], axis=1)
        second[r] = lax.dot_general(left, right, NT, preferred_element_type=F32).astype(BF)
    halves = []
    for half in range(2):
        at = 2 * zq + half
        scores = jnp.dot(self_t[...], hidden[at], preferred_element_type=F32)
        halves.append(scores + jnp.dot(neigh_t[...], second[at], preferred_element_type=F32))
    block = jnp.concatenate(halves, axis=1)[0 : out.shape[1]].astype(BF)
    for z in range(out.shape[0]):
        out[z] = block
    total = jnp.zeros((32, TILE), F32)
    for b in range(hidden.shape[0]):
        total = total + jnp.where(hidden[b, own, :].astype(F32) > 0.0, dhidden[b, own, :], 0.0)
    mine = jnp.sum(total, axis=1, keepdims=True)
    targets = jnp.concatenate([hidden[r, own, :] for r in range(tiles.shape[0])], axis=1)
    merged = jnp.concatenate([second[r, own, :] for r in range(tiles.shape[0])], axis=1)
    lane = lax.broadcasted_iota(jnp.int32, (32, 256), 1)
    first = lax.dot_general(targets, cot[...], NT, preferred_element_type=F32)
    first = jnp.where(lane == 255, mine, first)
    later = lax.dot_general(merged, cot[...], NT, preferred_element_type=F32)
    kept = jnp.where(core == 0, first, later)
    sent = jnp.where(core == 0, later, first)
    for half in range(2):
        keep[32 * half : 32 * half + 32, :] = kept[:, half * TILE : (half + 1) * TILE]
        send[32 * half : 32 * half + 32, :] = sent[:, half * TILE : (half + 1) * TILE]


def score(place, cols, hidden, dhidden, tiles, cot, self_t, neigh_t):
    shape = jax.ShapeDtypeStruct((64, TILE), F32)
    return pl.pallas_call(
        score_kernel,
        in_specs=[SMEM, SMEM] + [VMEM] * 6,
        out_specs=[VMEM] * 3,
        scratch_shapes=[pltpu.VMEM((tiles.shape[0], TILE, TILE), BF)],
        out_shape=[jax.ShapeDtypeStruct((8, 160, 256), BF), shape, shape],
        compiler_params=LIMIT,
    )(place, cols, hidden, dhidden, tiles, cot, self_t, neigh_t)


def total_kernel(parts, out):
    total = parts[0].astype(F32)
    for j in range(1, parts.shape[0]):
        total = total + parts[j].astype(F32)
    for d in range(out.shape[0]):
        out[d] = total.astype(BF)


def total(parts):
    return pl.pallas_call(
        total_kernel,
        in_specs=[VMEM],
        out_specs=VMEM,
        out_shape=jax.ShapeDtypeStruct((4,) + parts.shape[1:], BF),
        compiler_params=LIMIT,
    )(parts)


def logit_kernel(parts, out):
    classes = out.shape[0]
    for j in range(parts.shape[0]):
        out[:, 256 * j : 256 * (j + 1)] = parts[j].astype(F32)[0:classes]


def join(parts, classes):
    return pl.pallas_call(
        logit_kernel,
        in_specs=[VMEM],
        out_specs=VMEM,
        out_shape=jax.ShapeDtypeStruct((classes, 4 * parts.shape[2]), F32),
        compiler_params=LIMIT,
    )(parts)


def grad_kernel(
    place, hidden, dhidden, f0, f1, f2, e2, f3, g0, g1, g2, d2, g3, keep, send, total
):
    core, zr, y = place[0], place[3], place[4]
    blocks, deep, _ = f0.shape
    half = deep // 2
    total[...] = jnp.zeros_like(total)

    for side in range(2):
        first = side * (blocks // 2)
        far, twin = ((f2, g2), (e2, d2))[side]

        def grow(i, carry):
            b = first + i
            low = jnp.where(hidden[b].astype(F32) > 0.0, dhidden[b], 0.0).astype(BF)
            parts = [f0[b], f1[b], far[i], f3[b], g0[b], g1[b], twin[i], g3[b]]
            stack = jnp.concatenate(parts, axis=0)
            total[...] += lax.dot_general(stack, low, NT, preferred_element_type=F32)
            return carry

        lax.fori_loop(0, blocks // 2, grow, 0, unroll=4)
    for j in range(8):
        owner = 4 * (zr if j < 4 else 1 - zr) + lax.rem(y + 8 - j, 4)
        keep[owner] = total[pl.ds(pl.multiple_of(j * deep + core * half, 8), half), :]
        send[owner] = total[pl.ds(pl.multiple_of(j * deep + (1 - core) * half, 8), half), :]


def grad(place, hidden, dhidden, feats):
    _, deep, _ = feats[0].shape
    shape = jax.ShapeDtypeStruct((8, deep // 2, TILE), F32)
    return pl.pallas_call(
        grad_kernel,
        in_specs=[SMEM] + [VMEM] * 12,
        out_specs=[VMEM, VMEM],
        scratch_shapes=[pltpu.VMEM((8 * deep, TILE), F32)],
        out_shape=[shape, shape],
        compiler_params=LIMIT,
        cost_estimate=pl.CostEstimate(flops=10**9, bytes_accessed=7 * 10**6, transcendentals=0),
    )(place, hidden, dhidden, *feats)


def finish_kernel(place, keep, rest, grad_self, grad_neigh, head_self, head_neigh, bias):
    core = place[0]
    deep = grad_self.shape[0]
    classes = head_self.shape[1]
    first = jnp.where(core == 0, keep[...], rest[...])
    later = jnp.where(core == 0, rest[...], keep[...])
    for value, weight, head in ((first, grad_self, head_self), (later, grad_neigh, head_neigh)):
        for zq in range(4):
            for zr in range(2):
                pieces = [
                    value[(4 * zr + y) * deep : (4 * zr + y + 1) * deep, 32 * zq : 32 * zq + 32]
                    for y in range(4)
                ]
                at = (2 * zq + zr) * TILE
                weight[:, at : at + TILE] = jnp.concatenate(pieces, axis=1)
        base = 8 * deep
        head[:, 0:TILE] = value[base : base + 32]
        head[:, TILE:classes] = value[base + 32 : base + 64, 0 : classes - TILE]
    bias[...] = first[8 * deep + 32 : 8 * deep + 64].T[TILE - 1 : TILE]


def finish(place, keep, rest, deep, classes):
    weight = jax.ShapeDtypeStruct((deep, 1024), F32)
    head = jax.ShapeDtypeStruct((32, classes), F32)
    return pl.pallas_call(
        finish_kernel,
        in_specs=[SMEM, VMEM, VMEM],
        out_specs=[VMEM] * 5,
        out_shape=[weight, weight, head, head, jax.ShapeDtypeStruct((1, 32), F32)],
        compiler_params=LIMIT,
    )(place, keep, rest)


def shift(value, axis, by):
    return lax.ppermute(value, axis, [(i, (i + by) % 4) for i in range(4)])


def relay(value, near):
    half = value.shape[0] // 2
    far = [shift(near[0][:half], "y", 1), shift(near[1][half:], "y", 3)]
    return [value, near[0], *far, near[1]]


def swap(value, axis):
    return lax.ppermute(value, axis, [(0, 1), (1, 0)])


def shards(
    feature_table,
    node_ids,
    hop_cols,
    hop_tiles,
    target_cols,
    target_tiles,
    self_weight,
    neigh_weight,
    hidden_bias,
    head_self,
    head_neigh,
    batch_sizes,
    logit_cotangent,
):
    blocks = hop_cols.shape[0]
    deep = feature_table.shape[0]
    classes, target_rows = logit_cotangent.shape
    place = jnp.stack([lax.axis_index(axis) for axis in ("core", "x") + FEAT])

    packed, pair = pack(place, self_weight, neigh_weight, head_self, head_neigh)
    weights = lax.all_to_all(packed, FEAT, 0, 0, tiled=True)
    send, feats = hop(
        place, feature_table, node_ids, hop_cols, hidden_bias, hop_tiles, packed
    )
    peer = lax.ppermute(pair, "zq", [(0, 2), (2, 0), (1, 3), (3, 1)])
    weights, pair, peer, send, feats = lax.optimization_barrier(
        (weights, pair, peer, send, feats)
    )
    got = lax.all_to_all(send, FEAT, 0, 0, tiled=True)
    weights = weights.reshape(-1, 512)
    mine = [weights, shift(weights[:, :256], "x", 1), shift(weights[:, 256:], "x", 3)]

    mine, feats = lax.optimization_barrier((mine, feats))
    other = [swap(w, "core") for w in mine]
    twin = swap(feats, "zr")
    near = [shift(feats, "y", s) for s in (1, 3)]
    pair = jnp.concatenate([pair, peer], axis=0)
    quad = lax.ppermute(pair, "zq", [(0, 1), (1, 0), (2, 3), (3, 2)])

    hidden = layer(place, got, mine, other)
    twins = [shift(twin, "y", s) for s in (1, 3)]
    hidden, pair, quad, near, feats, twin, twins = lax.optimization_barrier(
        (hidden, pair, quad, near, feats, twin, twins)
    )
    hidden = lax.all_to_all(hidden, FEAT, 0, 0, tiled=True)
    feats = relay(feats, near) + relay(twin, twins)
    live = batch_sizes[lax.axis_index("x") * 2 + lax.axis_index("core")]
    ready = spread(place, target_cols, live, logit_cotangent, pair, quad, target_tiles, blocks)
    dhidden, cot, self_t, neigh_t = ready
    hidden, feats = lax.optimization_barrier((hidden, feats))

    scores, keep_head, send_head = score(
        place, target_cols, hidden, dhidden, target_tiles, cot, self_t, neigh_t
    )
    scores = lax.all_to_all(scores, ("zr", "y"), 0, 0, tiled=True)
    hidden, keep_head, send_head = lax.optimization_barrier((hidden, keep_head, send_head))
    keep_head = keep_head + swap(send_head, "core")
    keep, send = grad(place, hidden, dhidden, feats)
    keep = keep + swap(send, "core")
    keep, scores, keep_head = lax.optimization_barrier((keep, scores, keep_head))
    keep = lax.all_to_all(keep, ("zr", "y"), 0, 0, tiled=True)
    keep, scores = lax.optimization_barrier((keep, total(scores)))
    keep = jnp.concatenate([keep.reshape(-1, TILE), keep_head], axis=0)
    scores = lax.all_to_all(scores, "zq", 0, 0, tiled=True)
    keep = keep + lax.ppermute(keep, "x", [(0, 1), (1, 0), (2, 3), (3, 2)])
    keep = keep + lax.ppermute(keep, "x", [(0, 3), (3, 0), (1, 2), (2, 1)])
    results = finish(place, keep, swap(keep, "core"), deep, classes)
    return (join(scores, classes), *results[:4], results[4].reshape(-1))


def solution(mesh):
    split = Mesh(mesh.devices.reshape(4, 2, 4, 2, 4), DP + FEAT)
    return jax.shard_map(
        shards,
        mesh=split,
        in_specs=(
            P(FEAT, None),
            P(DP),
            P(DP, None),
            P(DP, None, None, None),
            P(DP, None),
            P(DP, None, None, None),
            P(FEAT, None),
            P(FEAT, None),
            P(FEAT),
            P(FEAT, None),
            P(FEAT, None),
            P(),
            P(None, DP),
        ),
        out_specs=(
            P(None, DP),
            P(FEAT, None),
            P(FEAT, None),
            P(FEAT, None),
            P(FEAT, None),
            P(FEAT),
        ),
        check_vma=False,
    )
```

```python
import jax
import jax.numpy as jnp
from jax import lax
from jax.experimental import pallas as pl
from jax.experimental.pallas import tpu as pltpu
from jax.sharding import Mesh, PartitionSpec as P

TILE = 128
FEAT = ("zq", "zr", "y")
DP = ("x", "core")
BF = jnp.bfloat16
F32 = jnp.float32
NT = (((1,), (1,)), ((), ()))
VMEM = pl.BlockSpec(memory_space=pltpu.VMEM)
SMEM = pl.BlockSpec(memory_space=pltpu.SMEM)
HBM = pl.BlockSpec(memory_space=pl.ANY)
LIMIT = pltpu.CompilerParams(vmem_limit_bytes=56 * 2**20)


def aligned(index, size):
    return pl.ds(pl.multiple_of(index * size, size), size)


def split_bias(bias):
    row = lax.broadcasted_iota(jnp.int32, (8, bias.shape[1]), 0)
    left = jnp.broadcast_to(bias, row.shape)
    high = left.astype(BF).astype(F32)
    left = left - high
    middle = left.astype(BF).astype(F32)
    low = left - middle
    return jnp.where(row == 0, high, jnp.where(row == 1, middle, jnp.where(row == 2, low, 0.0)))


def hop_kernel(place, ids, cols, table, bias, tiles_hbm, _, out, feats, rows, picked, tiles, sem):
    width = table.shape[0]
    blocks = tiles.shape[0]
    group = blocks // 8
    copies = [
        pltpu.make_async_copy(
            tiles_hbm.at[pl.ds(j * group, group)], tiles.at[pl.ds(j * group, group)], sem.at[j]
        )
        for j in range(8)
    ]
    for copy in copies:
        copy.start()

    def turn(b, carry):
        rows[aligned(b, TILE), 0:width] = table[:, aligned(b, TILE)].astype(F32).T
        return carry

    lax.fori_loop(0, table.shape[1] // TILE, turn, 0, unroll=16)
    step = 64

    def pick(g, carry):
        base = pl.multiple_of(g * step, step)
        for u in range(step):
            picked[pl.ds(base + u, 1), :] = rows[pl.ds(ids[base + u], 1), :]
        return carry

    lax.fori_loop(0, ids.shape[0] // step, pick, 0)
    lane = lax.broadcasted_iota(jnp.int32, (8, TILE), 1)
    term = split_bias(jnp.concatenate([bias[...]] * 4, axis=1))
    term = jnp.where(lane // 32 == place[4], term, 0.0)
    for copy in copies:
        copy.wait()

    def merge(r, carry):
        own = picked[aligned(r, TILE), :].T[0:width]
        left = jnp.concatenate([tiles[r, k] for k in range(8)], axis=1)
        right = jnp.concatenate(
            [picked[aligned(cols[r, k], TILE), :].astype(BF) for k in range(8)], axis=0
        )
        total = jnp.dot(left, right, preferred_element_type=F32)
        both = jnp.concatenate([own, total.T[0:width]], axis=0)
        feats[r] = both.astype(BF)
        out[r] = jnp.concatenate([both, term], axis=0).astype(BF)
        return carry

    lax.fori_loop(0, blocks, merge, 0, unroll=4)


def hop(place, table, ids, cols, bias, tiles, after):
    blocks, deep = tiles.shape[0], 2 * table.shape[0]
    return pl.pallas_call(
        hop_kernel,
        in_specs=[SMEM, SMEM, SMEM, VMEM, VMEM, HBM, HBM],
        out_specs=[VMEM, VMEM],
        scratch_shapes=[
            pltpu.VMEM((table.shape[1], TILE), F32),
            pltpu.VMEM((ids.shape[0], TILE), F32),
            pltpu.VMEM(tiles.shape, BF),
            pltpu.SemaphoreType.DMA((8,)),
        ],
        out_shape=[
            jax.ShapeDtypeStruct((blocks, deep + 8, TILE), BF),
            jax.ShapeDtypeStruct((blocks, deep, TILE), BF),
        ],
        compiler_params=LIMIT,
        cost_estimate=pl.CostEstimate(flops=10**9, bytes_accessed=60 * 10**6, transcendentals=0),
    )(place, ids, cols, table, bias.reshape(1, -1), tiles, after)


def pack_kernel(place, own, neigh, head_self, head_neigh, weights, heads):
    core, x = place[0], place[1]
    cols = aligned(lax.rem(x, 2), 512)
    block = jnp.where(core == 0, own[:, cols].astype(F32), neigh[:, cols].astype(F32)).astype(BF)
    for d in range(weights.shape[0]):
        weights[d] = block
    classes = head_self.shape[1]
    heads[...] = jnp.zeros_like(heads)
    heads[0:32, 0:classes] = head_self[...]
    heads[32:64, 0:classes] = head_neigh[...]


def pack(place, own, neigh, head_self, head_neigh):
    return pl.pallas_call(
        pack_kernel,
        in_specs=[SMEM] + [VMEM] * 4,
        out_specs=[VMEM, VMEM],
        out_shape=[
            jax.ShapeDtypeStruct((32, own.shape[0], 512), BF),
            jax.ShapeDtypeStruct((64, 256), BF),
        ],
        compiler_params=LIMIT,
    )(place, own, neigh, head_self, head_neigh)


def spread_kernel(
    place, cols, live, logit_cot, pair, quad, tiles, out, cot, self_t, neigh_t, own, neigh
):
    classes, slots = logit_cot.shape
    lane = lax.broadcasted_iota(jnp.int32, (classes, slots), 1)
    kept = jnp.where(lane < live[0], logit_cot[...].astype(F32), 0.0)
    cot[...] = jnp.concatenate([kept, jnp.zeros((256 - classes, slots), F32)], axis=0).astype(BF)
    out[...] = jnp.zeros_like(out)
    zq = place[2]
    low, high = 2 * (zq // 2), 2 - 2 * (zq // 2)
    odd = lax.rem(zq, 2)
    for part, first in ((pair, low), (quad, high)):
        for j, at in enumerate((first + odd, first + 1 - odd)):
            own[aligned(at, 32), :] = part[64 * j : 64 * j + 32]
            neigh[aligned(at, 32), :] = part[64 * j + 32 : 64 * j + 64]
    self_t[...] = own[...].astype(F32).T.astype(BF)
    neigh_t[...] = neigh[...].astype(F32).T.astype(BF)
    for r in range(tiles.shape[0]):
        part = cot[:, r * TILE : (r + 1) * TILE]
        out[r] = jnp.dot(own[...], part, preferred_element_type=F32)
    for r in range(tiles.shape[0]):
        part = cot[:, r * TILE : (r + 1) * TILE]
        back = jnp.dot(neigh[...], part, preferred_element_type=F32).astype(BF)
        for k in range(8):
            out[cols[r, k]] += jnp.dot(back, tiles[r, k], preferred_element_type=F32)


def spread(place, cols, live, logit_cot, pair, quad, tiles, blocks):
    return pl.pallas_call(
        spread_kernel,
        in_specs=[SMEM, SMEM, SMEM] + [VMEM] * 4,
        out_specs=[VMEM] * 4,
        scratch_shapes=[pltpu.VMEM((TILE, 256), BF)] * 2,
        out_shape=[
            jax.ShapeDtypeStruct((blocks, TILE, TILE), F32),
            jax.ShapeDtypeStruct((256, logit_cot.shape[1]), BF),
            jax.ShapeDtypeStruct((256, TILE), BF),
            jax.ShapeDtypeStruct((256, TILE), BF),
        ],
        compiler_params=LIMIT,
        cost_estimate=pl.CostEstimate(flops=10**9, bytes_accessed=8 * 10**6, transcendentals=0),
    )(place, cols, live.reshape(1), logit_cot, pair, quad, tiles)


def layer_kernel(place, got, w0, w1, w2, o0, o1, o2, out, mine, other):
    core, x = place[0], place[1]
    deep = w0.shape[0] // 32
    for j in range(8):
        pieces = [got[4 * j + i].astype(F32) for i in range(4)]
        own = jnp.concatenate([piece[0:deep] for piece in pieces], axis=0).T.astype(BF)
        agg = jnp.concatenate([piece[deep : 2 * deep] for piece in pieces], axis=0).T.astype(BF)
        at = slice(j * 4 * deep, (j + 1) * 4 * deep)
        mine[:, at] = jnp.where(core == 0, own, agg)
        other[:, at] = jnp.where(core == 0, agg, own)

    def emit(chunk, w, o):
        preact = jnp.dot(mine[...], w, preferred_element_type=F32)
        preact = preact + jnp.dot(other[...], o, preferred_element_type=F32)
        rows = aligned(chunk, 32)
        for half in range(2):
            z = 2 * chunk + half
            terms = sum(got[4 * z + i].astype(F32)[2 * deep :] for i in range(4))
            bias = jnp.sum(terms, axis=0, keepdims=True)
            hidden = jnp.maximum(preact[:, half * TILE : (half + 1) * TILE] + bias, 0.0)
            hidden = hidden.T.astype(BF)
            for y in range(4):
                for zq in range(4):
                    out[8 * zq + 4 * half + y, rows, :] = hidden[32 * y : 32 * y + 32]

    near = 2 * lax.rem(x, 2)
    far = 2 - near
    emit(near, w0[:, 0:256], o0[:, 0:256])
    emit(near + 1, w0[:, 256:512], o0[:, 256:512])
    emit(far, w1[...], o1[...])
    emit(far + 1, w2[...], o2[...])


def layer(place, got, mine, other):
    return pl.pallas_call(
        layer_kernel,
        in_specs=[SMEM] + [VMEM] * 7,
        out_specs=VMEM,
        scratch_shapes=[pltpu.VMEM((TILE, mine[0].shape[0]), BF)] * 2,
        out_shape=jax.ShapeDtypeStruct((32, TILE, TILE), BF),
        compiler_params=LIMIT,
    )(place, got, *mine, *other)


def score_kernel(
    place, cols, hidden, dhidden, tiles, cot, self_t, neigh_t, out, keep, send, second
):
    core, zq = place[0], place[2]
    own = aligned(zq, 32)
    for r in range(tiles.shape[0]):
        left = jnp.concatenate([hidden[cols[r, k]] for k in range(8)], axis=1)
        right = jnp.concatenate([tiles[r, k] for k in range(8)], axis=1)
        second[r] = lax.dot_general(left, right, NT, preferred_element_type=F32).astype(BF)
    halves = []
    for half in range(2):
        at = 2 * zq + half
        scores = jnp.dot(self_t[...], hidden[at], preferred_element_type=F32)
        halves.append(scores + jnp.dot(neigh_t[...], second[at], preferred_element_type=F32))
    block = jnp.concatenate(halves, axis=1)[0 : out.shape[1]].astype(BF)
    for z in range(out.shape[0]):
        out[z] = block
    total = jnp.zeros((32, TILE), F32)
    for b in range(hidden.shape[0]):
        total = total + jnp.where(hidden[b, own, :].astype(F32) > 0.0, dhidden[b, own, :], 0.0)
    mine = jnp.sum(total, axis=1, keepdims=True)
    targets = jnp.concatenate([hidden[r, own, :] for r in range(tiles.shape[0])], axis=1)
    merged = jnp.concatenate([second[r, own, :] for r in range(tiles.shape[0])], axis=1)
    lane = lax.broadcasted_iota(jnp.int32, (32, 256), 1)
    first = lax.dot_general(targets, cot[...], NT, preferred_element_type=F32)
    first = jnp.where(lane == 255, mine, first)
    later = lax.dot_general(merged, cot[...], NT, preferred_element_type=F32)
    kept = jnp.where(core == 0, first, later)
    sent = jnp.where(core == 0, later, first)
    for half in range(2):
        keep[32 * half : 32 * half + 32, :] = kept[:, half * TILE : (half + 1) * TILE]
        send[32 * half : 32 * half + 32, :] = sent[:, half * TILE : (half + 1) * TILE]


def score(place, cols, hidden, dhidden, tiles, cot, self_t, neigh_t):
    shape = jax.ShapeDtypeStruct((64, TILE), F32)
    return pl.pallas_call(
        score_kernel,
        in_specs=[SMEM, SMEM] + [VMEM] * 6,
        out_specs=[VMEM] * 3,
        scratch_shapes=[pltpu.VMEM((tiles.shape[0], TILE, TILE), BF)],
        out_shape=[jax.ShapeDtypeStruct((8, 160, 256), BF), shape, shape],
        compiler_params=LIMIT,
    )(place, cols, hidden, dhidden, tiles, cot, self_t, neigh_t)


def total_kernel(parts, out):
    total = parts[0].astype(F32)
    for j in range(1, parts.shape[0]):
        total = total + parts[j].astype(F32)
    for d in range(out.shape[0]):
        out[d] = total.astype(BF)


def total(parts):
    return pl.pallas_call(
        total_kernel,
        in_specs=[VMEM],
        out_specs=VMEM,
        out_shape=jax.ShapeDtypeStruct((4,) + parts.shape[1:], BF),
        compiler_params=LIMIT,
    )(parts)


def logit_kernel(parts, out):
    classes = out.shape[0]
    for j in range(parts.shape[0]):
        out[:, 256 * j : 256 * (j + 1)] = parts[j].astype(F32)[0:classes]


def join(parts, classes):
    return pl.pallas_call(
        logit_kernel,
        in_specs=[VMEM],
        out_specs=VMEM,
        out_shape=jax.ShapeDtypeStruct((classes, 4 * parts.shape[2]), F32),
        compiler_params=LIMIT,
    )(parts)


def grad_kernel(
    place, hidden, dhidden, f0, f1, f2, e2, f3, g0, g1, g2, d2, g3, keep, send, total
):
    core, zr, y = place[0], place[3], place[4]
    blocks, deep, _ = f0.shape
    half = deep // 2
    total[...] = jnp.zeros_like(total)

    for side in range(2):
        first = side * (blocks // 2)
        far, twin = ((f2, g2), (e2, d2))[side]

        def grow(i, carry):
            b = first + i
            low = jnp.where(hidden[b].astype(F32) > 0.0, dhidden[b], 0.0).astype(BF)
            parts = [f0[b], f1[b], far[i], f3[b], g0[b], g1[b], twin[i], g3[b]]
            stack = jnp.concatenate(parts, axis=0)
            total[...] += lax.dot_general(stack, low, NT, preferred_element_type=F32)
            return carry

        lax.fori_loop(0, blocks // 2, grow, 0, unroll=4)
    for j in range(8):
        owner = 4 * (zr if j < 4 else 1 - zr) + lax.rem(y + 8 - j, 4)
        keep[owner] = total[pl.ds(pl.multiple_of(j * deep + core * half, 8), half), :]
        send[owner] = total[pl.ds(pl.multiple_of(j * deep + (1 - core) * half, 8), half), :]


def grad(place, hidden, dhidden, feats):
    _, deep, _ = feats[0].shape
    shape = jax.ShapeDtypeStruct((8, deep // 2, TILE), F32)
    return pl.pallas_call(
        grad_kernel,
        in_specs=[SMEM] + [VMEM] * 12,
        out_specs=[VMEM, VMEM],
        scratch_shapes=[pltpu.VMEM((8 * deep, TILE), F32)],
        out_shape=[shape, shape],
        compiler_params=LIMIT,
        cost_estimate=pl.CostEstimate(flops=10**9, bytes_accessed=7 * 10**6, transcendentals=0),
    )(place, hidden, dhidden, *feats)


def finish_kernel(place, keep, rest, grad_self, grad_neigh, head_self, head_neigh, bias):
    core = place[0]
    deep = grad_self.shape[0]
    classes = head_self.shape[1]
    first = jnp.where(core == 0, keep[...], rest[...])
    later = jnp.where(core == 0, rest[...], keep[...])
    for value, weight, head in ((first, grad_self, head_self), (later, grad_neigh, head_neigh)):
        for zq in range(4):
            for zr in range(2):
                pieces = [
                    value[(4 * zr + y) * deep : (4 * zr + y + 1) * deep, 32 * zq : 32 * zq + 32]
                    for y in range(4)
                ]
                at = (2 * zq + zr) * TILE
                weight[:, at : at + TILE] = jnp.concatenate(pieces, axis=1)
        base = 8 * deep
        head[:, 0:TILE] = value[base : base + 32]
        head[:, TILE:classes] = value[base + 32 : base + 64, 0 : classes - TILE]
    bias[...] = first[8 * deep + 32 : 8 * deep + 64].T[TILE - 1 : TILE]


def finish(place, keep, rest, deep, classes):
    weight = jax.ShapeDtypeStruct((deep, 1024), F32)
    head = jax.ShapeDtypeStruct((32, classes), F32)
    return pl.pallas_call(
        finish_kernel,
        in_specs=[SMEM, VMEM, VMEM],
        out_specs=[VMEM] * 5,
        out_shape=[weight, weight, head, head, jax.ShapeDtypeStruct((1, 32), F32)],
        compiler_params=LIMIT,
    )(place, keep, rest)


def shift(value, axis, by):
    return lax.ppermute(value, axis, [(i, (i + by) % 4) for i in range(4)])


def relay(value, near):
    half = value.shape[0] // 2
    far = [shift(near[0][:half], "y", 1), shift(near[1][half:], "y", 3)]
    return [value, near[0], *far, near[1]]


def swap(value, axis):
    return lax.ppermute(value, axis, [(0, 1), (1, 0)])


def shards(
    feature_table,
    node_ids,
    hop_cols,
    hop_tiles,
    target_cols,
    target_tiles,
    self_weight,
    neigh_weight,
    hidden_bias,
    head_self,
    head_neigh,
    batch_sizes,
    logit_cotangent,
):
    blocks = hop_cols.shape[0]
    deep = feature_table.shape[0]
    classes, target_rows = logit_cotangent.shape
    place = jnp.stack([lax.axis_index(axis) for axis in ("core", "x") + FEAT])

    packed, pair = pack(place, self_weight, neigh_weight, head_self, head_neigh)
    weights = lax.all_to_all(packed, FEAT, 0, 0, tiled=True)
    send, feats = hop(
        place, feature_table, node_ids, hop_cols, hidden_bias, hop_tiles, packed
    )
    peer = lax.ppermute(pair, "zq", [(0, 1), (1, 0), (2, 3), (3, 2)])
    weights, pair, peer, send, feats = lax.optimization_barrier(
        (weights, pair, peer, send, feats)
    )
    got = lax.all_to_all(send, FEAT, 0, 0, tiled=True)
    weights = weights.reshape(-1, 512)
    mine = [weights, shift(weights[:, :256], "x", 1), shift(weights[:, 256:], "x", 3)]

    mine, feats = lax.optimization_barrier((mine, feats))
    other = [swap(w, "core") for w in mine]
    twin = swap(feats, "zr")
    near = [shift(feats, "y", s) for s in (1, 3)]
    pair = jnp.concatenate([pair, peer], axis=0)
    quad = lax.ppermute(pair, "zq", [(0, 2), (2, 0), (1, 3), (3, 1)])

    hidden = layer(place, got, mine, other)
    hidden, pair, quad, near, feats, twin = lax.optimization_barrier(
        (hidden, pair, quad, near, feats, twin)
    )
    hidden = lax.all_to_all(hidden, FEAT, 0, 0, tiled=True)
    feats = relay(feats, near)
    near = [shift(twin, "y", s) for s in (1, 3)]
    live = batch_sizes[lax.axis_index("x") * 2 + lax.axis_index("core")]
    ready = spread(place, target_cols, live, logit_cotangent, pair, quad, target_tiles, blocks)
    ready, near = lax.optimization_barrier((ready, near))
    dhidden, cot, self_t, neigh_t = ready
    feats = feats + relay(twin, near)
    hidden, feats = lax.optimization_barrier((hidden, feats))

    scores, keep_head, send_head = score(
        place, target_cols, hidden, dhidden, target_tiles, cot, self_t, neigh_t
    )
    scores = lax.all_to_all(scores, ("zr", "y"), 0, 0, tiled=True)
    hidden, keep_head, send_head = lax.optimization_barrier((hidden, keep_head, send_head))
    keep_head = keep_head + swap(send_head, "core")
    keep, send = grad(place, hidden, dhidden, feats)
    keep = keep + swap(send, "core")
    keep, scores, keep_head = lax.optimization_barrier((keep, scores, keep_head))
    keep = lax.all_to_all(keep, ("zr", "y"), 0, 0, tiled=True)
    keep, scores = lax.optimization_barrier((keep, total(scores)))
    keep = jnp.concatenate([keep.reshape(-1, TILE), keep_head], axis=0)
    scores = lax.all_to_all(scores, "zq", 0, 0, tiled=True)
    keep = keep + lax.ppermute(keep, "x", [(0, 1), (1, 0), (2, 3), (3, 2)])
    keep = keep + lax.ppermute(keep, "x", [(0, 3), (3, 0), (1, 2), (2, 1)])
    results = finish(place, keep, swap(keep, "core"), deep, classes)
    return (join(scores, classes), *results[:4], results[4].reshape(-1))


def solution(mesh):
    split = Mesh(mesh.devices.reshape(4, 2, 4, 2, 4), DP + FEAT)
    return jax.shard_map(
        shards,
        mesh=split,
        in_specs=(
            P(FEAT, None),
            P(DP),
            P(DP, None),
            P(DP, None, None, None),
            P(DP, None),
            P(DP, None, None, None),
            P(FEAT, None),
            P(FEAT, None),
            P(FEAT),
            P(FEAT, None),
            P(FEAT, None),
            P(),
            P(None, DP),
        ),
        out_specs=(
            P(None, DP),
            P(FEAT, None),
            P(FEAT, None),
            P(FEAT, None),
            P(FEAT, None),
            P(FEAT),
        ),
        check_vma=False,
    )
```
